128 devices in a mesh: row: 8 (over y, core), col: 8 (over z, x_lo), ch: 2 (over x_hi).
Axes of the slice: x: 4 (x_hi: 2, x_lo: 2; x = x_hi * 2 + x_lo), y: 4, z: 4, core: 2. Of those that a mesh axis runs over, the one named last changes fastest.
Arguments:
- pair: bfloat16 [896, 896, 128], P('row', 'col'), may hold values from -6 to 6
- pair_mask: int32 [896, 896], P('row', 'col'), may hold values 0 or 1
- ln_in_gain: float32 [128], replicated, may hold values from 0.1 to 1.9
- w_left_gate: bfloat16 [128, 128], P(None, 'ch'), may hold values from -0.5 to 0.5
- w_left_proj: bfloat16 [128, 128], P(None, 'ch'), may hold values from -0.5 to 0.5
- w_right_gate: bfloat16 [128, 128], P(None, 'ch'), may hold values from -0.5 to 0.5
- w_right_proj: bfloat16 [128, 128], P(None, 'ch'), may hold values from -0.5 to 0.5
- w_gate: bfloat16 [128, 128], replicated, may hold values from -0.5 to 0.5
- ln_out_gain: float32 [128], replicated, may hold values from 0.1 to 1.9
- w_out: bfloat16 [128, 128], replicated, may hold values from -0.5 to 0.5
Outputs:
- update: bfloat16 [896, 896, 128], P('row', ('col', 'ch'))
The draws below stay inside these ranges and needn't reach their ends.
All inputs are finite; a program needn't handle non-finite values. No bound on the sum of `pair_mask` on one device may be relied on, other than what follows from the above.
Results may differ from the reference program's by a relative error of at most 0.025.
Values may be sent and summed in bfloat16 or wider, within the bound.
No kernel may reach another device: no remote copies, remote signals or barrier semaphores. Data moves between devices by JAX's collectives and lax.ppermute only.
A program may use at most 192 MiB of HBM per device.

```python
import jax
import jax.numpy as jnp
from jax import lax

C = 128
CH = 128
N = 896


def touch_ends(result, key, low, high):
    place = [jax.random.randint(jax.random.fold_in(key, axis), (), 0, length) for axis, length in enumerate(result.shape)]
    longest = result.shape.index(max(result.shape))
    neighbour = place[:longest] + [(place[longest] + 1) % result.shape[longest]] + place[longest + 1:]
    return result.at[tuple(place)].set(low).at[tuple(neighbour)].set(high)


def level_of(rng, shape, shards, least, top_value):
    factor_of, own = 1.0, jax.random.fold_in(rng, 6)
    for position, parts in shards:
        steps = jnp.exp(jax.random.uniform(jax.random.fold_in(own, position), (parts,), jnp.float32, least / len(shards), top_value / len(shards)))
        factor_of = factor_of * jnp.repeat(steps, shape[position] // parts).reshape([-1 if axis == position else 1 for axis in range(len(shape))])
    return factor_of


def gaussian(key, shape, scale, bound, split=(), held_as=jnp.bfloat16):
    values = scale * jax.random.normal(key, shape, jnp.float32)
    if split:
        values = values * level_of(key, shape, split, -0.22, 0.18)
    return jnp.clip(values, -bound, bound).astype(held_as)


def setup_inputs(seed: int = 0) -> dict:
    key_of = jax.random.split(jax.random.key(seed), 11)
    return {
        "pair": gaussian(key_of[0], (N, N, C), 1.0, 6.0, ((0, 8), (1, 8))),
        "pair_mask": touch_ends((jax.random.randint(key_of[1], (N, N), 0, 10) < 9).astype(jnp.int32), jax.random.fold_in(key_of[1], 1), 0, 1),
        "ln_in_gain": jnp.clip(1.0 + 0.18 * jax.random.normal(key_of[2], (C,), jnp.float32), 0.1, 1.9),
        "w_left_gate": gaussian(key_of[3], (C, CH), C ** -0.5, 0.5, ((1, 2),)),
        "w_left_proj": gaussian(key_of[4], (C, CH), C ** -0.5, 0.5, ((1, 2),)),
        "w_right_gate": gaussian(key_of[5], (C, CH), C ** -0.5, 0.5, ((1, 2),)),
        "w_right_proj": gaussian(key_of[6], (C, CH), C ** -0.5, 0.5, ((1, 2),)),
        "w_gate": gaussian(key_of[7], (C, C), C ** -0.5, 0.5),
        "ln_out_gain": jnp.clip(1.0 + 0.18 * jax.random.normal(key_of[8], (CH,), jnp.float32), 0.1, 1.9),
        "w_out": gaussian(key_of[9], (CH, C), CH ** -0.5, 0.5),
    }


epsilon = 1e-05

def normalize(values, gain_vec):
    center_val = lax.optimization_barrier(jnp.mean(values, axis=-1, keepdims=True))
    centered = values - center_val
    spread = lax.optimization_barrier(jnp.mean(centered * centered, axis=-1, keepdims=True))
    return centered * lax.rsqrt(spread + epsilon) * gain_vec

def reference(pair, pair_mask, ln_in_gain, w_left_gate, w_left_proj, w_right_gate, w_right_proj, w_gate, ln_out_gain, w_out):
    pair_normed = normalize(pair.astype(jnp.float32), ln_in_gain.astype(jnp.float32)).astype(jnp.bfloat16)
    valid_pairs = pair_mask.astype(jnp.float32)[:, :, None]

    def project(weight):
        return jnp.dot(pair_normed, weight, preferred_element_type=jnp.float32)
    left_vals = (valid_pairs * jax.nn.sigmoid(project(w_left_gate)) * project(w_left_proj)).astype(jnp.bfloat16)
    right_vals = (valid_pairs * jax.nn.sigmoid(project(w_right_gate)) * project(w_right_proj)).astype(jnp.bfloat16)
    gate_vals = jax.nn.sigmoid(project(w_gate))
    group_size = 16 if CH % 16 == 0 else CH
    pieces_list = []
    for first_chan in range(0, CH, group_size):
        left_part = left_vals[:, :, first_chan:first_chan + group_size].astype(jnp.float32)
        right_part = right_vals[:, :, first_chan:first_chan + group_size].astype(jnp.float32)
        pieces_list.append(jnp.einsum('kic,kjc->ijc', left_part, right_part))
    hidden = jnp.concatenate(pieces_list, axis=2)
    hidden_normed = normalize(hidden, ln_out_gain.astype(jnp.float32)).astype(jnp.bfloat16)
    projected = jnp.dot(hidden_normed, w_out, preferred_element_type=jnp.float32)
    return (gate_vals * projected).astype(jnp.bfloat16)
```

```python
import jax
import jax.numpy as jnp
from jax import lax
from jax.experimental import pallas as pl
from jax.experimental.pallas import tpu as pltpu
from jax.sharding import PartitionSpec as P

epsilon = 1e-05
f32 = jnp.float32
bf16 = jnp.bfloat16
lanes = 128
chunk = 16


def sigmoid(values):
    return 0.5 * jnp.tanh(0.5 * values) + 0.5


def project_kernel(
    pair_ref,
    mask_ref,
    gain_ref,
    left_gate_ref,
    left_proj_ref,
    right_gate_ref,
    right_proj_ref,
    gate_weight_ref,
    message_ref,
    gate_ref,
    weight_scr,
    normed_scr,
    mask_scr,
    turn_scr,
):
    tile = pair_ref.shape[1]
    part = left_gate_ref.shape[1]
    half = tile // 2

    @pl.when(pl.program_id(0) == 0)
    def _():
        joined = jnp.concatenate(
            [left_gate_ref[...], left_proj_ref[...], right_gate_ref[...], right_proj_ref[...]],
            axis=1,
        )
        weight_scr[...] = joined.astype(f32).T.astype(bf16)
        normed_scr[...] = jnp.zeros_like(normed_scr)
        mask_scr[...] = jnp.zeros_like(mask_scr)

    values = pair_ref[...].astype(f32)
    centered = values - jnp.mean(values, axis=-1, keepdims=True)
    spread = jnp.mean(centered * centered, axis=-1, keepdims=True)
    normed = centered * lax.rsqrt(spread + epsilon) * gain_ref[...][None]
    normed_scr[:, :tile, :] = normed.astype(bf16)
    mask_scr[:, :tile] = mask_ref[...].astype(f32)

    own = jnp.where(lax.axis_index("ch") == 0, normed[:, :half], normed[:, half:])
    own = own.reshape(chunk * half, lanes).astype(bf16)
    gate = sigmoid(jnp.dot(own, gate_weight_ref[...], preferred_element_type=f32))
    gate_ref[...] = gate.reshape(gate_ref.shape)

    for k in range(0, chunk, 2):
        source = normed_scr[k : k + 2].reshape(2 * lanes, lanes)
        products = lax.dot_general(
            weight_scr[...], source, (((1,), (1,)), ((), ())), preferred_element_type=f32
        )
        for kk in range(2):
            own_lanes = products[:, kk * lanes : (kk + 1) * lanes]
            valid = mask_scr[k + kk : k + kk + 1, :]
            for side in range(2):
                base = 2 * part * side
                vals = (
                    valid
                    * sigmoid(own_lanes[base : base + part])
                    * own_lanes[base + part : base + 2 * part]
                )
                turn_scr[side, pl.ds(k + kk, part, stride=chunk), :] = vals
    for side in range(2):
        message_ref[:, side] = turn_scr[side].reshape(part, chunk, lanes).astype(bf16)


def product_kernel(left_ref, right_ref, out_ref, right_scr):
    rows, cols = right_ref.shape[0], right_ref.shape[1]
    tile = right_ref.shape[3]
    depth = rows * tile

    @pl.when(pl.program_id(0) == 0)
    def _():
        for q in range(cols):
            block = right_ref[:, q, 0].reshape(depth, lanes)
            right_scr[q * tile : (q + 1) * tile, :] = block.astype(f32).T[:tile].astype(bf16)

    sides = [left_ref[:, p, 0].reshape(depth, lanes) for p in range(left_ref.shape[1])]
    hidden = jnp.dot(
        right_scr[...], jnp.concatenate(sides, axis=1), preferred_element_type=f32
    ).astype(bf16)
    for p in range(left_ref.shape[1]):
        out_ref[p] = hidden[:, p * lanes : (p + 1) * lanes]


def finish_kernel(hidden_ref, gate_ref, gain_ref, weight_ref, out_ref, weight_scr, turn_scr, out_scr):
    channels = hidden_ref.shape[0]
    tile = out_ref.shape[0]

    @pl.when(pl.program_id(0) == 0)
    def _():
        spread_gain = jnp.broadcast_to(gain_ref[...], (channels, channels)).T
        scaled = spread_gain * weight_ref[...].astype(f32)
        part = channels // 2
        for side in range(2):
            turn_scr[pl.ds(side, part, stride=2), :] = scaled[side * part : (side + 1) * part]
        weight_scr[...] = turn_scr[:channels, :].astype(bf16)

    hidden = hidden_ref[:, 0].astype(f32)
    centered = hidden - jnp.mean(hidden, axis=0, keepdims=True)
    spread = jnp.mean(centered * centered, axis=0, keepdims=True)
    normed = centered * lax.rsqrt(spread + epsilon)
    turn_scr[...] = normed.reshape(channels * 8, lanes)
    for j in range(8):
        row = turn_scr[pl.ds(j, channels, stride=8), :].astype(bf16)
        projected = lax.dot_general(
            row, weight_scr[...], (((0,), (0,)), ((), ())), preferred_element_type=f32
        )
        out_scr[pl.ds(j, tile, stride=8), :] = projected[:tile]
    out_ref[:, 0] = (out_scr[...].reshape(tile, 8, lanes) * gate_ref[:, 0]).astype(bf16)


def shards(
    pair,
    pair_mask,
    ln_in_gain,
    w_left_gate,
    w_left_proj,
    w_right_gate,
    w_right_proj,
    w_gate,
    ln_out_gain,
    w_out,
):
    tile, channels = pair.shape[0], pair.shape[2]
    part = w_left_gate.shape[1]
    rows, cols, ch = lax.axis_size("row"), lax.axis_size("col"), lax.axis_size("ch")
    half = tile // ch
    groups = half // 8
    whole = lambda shape: pl.BlockSpec(shape, lambda s: (0,) * len(shape))

    message, gate = pl.pallas_call(
        project_kernel,
        grid=(tile // chunk,),
        in_specs=[
            pl.BlockSpec((chunk, tile, channels), lambda s: (s, 0, 0)),
            pl.BlockSpec((chunk, tile), lambda s: (s, 0)),
            whole((1, channels)),
            whole((channels, part)),
            whole((channels, part)),
            whole((channels, part)),
            whole((channels, part)),
            whole((channels, channels)),
        ],
        out_specs=[
            pl.BlockSpec((part, 2, chunk, lanes), lambda s: (0, 0, s, 0)),
            pl.BlockSpec((chunk, groups, 8, lanes), lambda s: (s, 0, 0, 0)),
        ],
        out_shape=[
            jax.ShapeDtypeStruct((part, 2, tile, lanes), bf16),
            jax.ShapeDtypeStruct((tile, groups, 8, lanes), f32),
        ],
        scratch_shapes=[
            pltpu.VMEM((4 * part, channels), bf16),
            pltpu.VMEM((chunk, lanes, channels), bf16),
            pltpu.VMEM((chunk, lanes), f32),
            pltpu.VMEM((2, part * chunk, lanes), f32),
        ],
        compiler_params=pltpu.CompilerParams(vmem_limit_bytes=24 * 2**20),
        name="project",
    )(
        pair,
        pair_mask,
        ln_in_gain.reshape(1, channels),
        w_left_gate,
        w_left_proj,
        w_right_gate,
        w_right_proj,
        w_gate,
    )

    received = lax.all_to_all(message, ("row", "col"), 0, 0, tiled=True)
    received = received.reshape(rows, cols, 2, tile, lanes)

    pairs = 2
    hidden = pl.pallas_call(
        product_kernel,
        grid=(rows // pairs,),
        in_specs=[
            pl.BlockSpec((rows, pairs, 1, tile, lanes), lambda s: (0, s, 0, 0, 0)),
            pl.BlockSpec((rows, cols, 1, tile, lanes), lambda s: (0, 0, 1, 0, 0)),
        ],
        out_specs=pl.BlockSpec((pairs, cols * tile, lanes), lambda s: (s, 0, 0)),
        out_shape=jax.ShapeDtypeStruct((rows, cols * tile, lanes), bf16),
        scratch_shapes=[pltpu.VMEM((cols * tile, rows * tile), bf16)],
        compiler_params=pltpu.CompilerParams(vmem_limit_bytes=24 * 2**20),
        name="product",
    )(received, received)

    parts = lax.all_to_all(
        hidden.reshape(rows * cols * ch, half, lanes), ("row", "col", "ch"), 0, 0, tiled=True
    )
    parts = parts.reshape(channels, groups, 8, lanes)

    update = pl.pallas_call(
        finish_kernel,
        grid=(groups,),
        in_specs=[
            pl.BlockSpec((channels, 1, 8, lanes), lambda s: (0, s, 0, 0)),
            pl.BlockSpec((tile, 1, 8, lanes), lambda s: (0, s, 0, 0)),
            whole((1, channels)),
            whole((channels, channels)),
        ],
        out_specs=pl.BlockSpec((tile, 1, 8, lanes), lambda s: (0, s, 0, 0)),
        out_shape=jax.ShapeDtypeStruct((tile, groups, 8, lanes), bf16),
        scratch_shapes=[
            pltpu.VMEM((channels, channels), bf16),
            pltpu.VMEM((channels * 8, lanes), f32),
            pltpu.VMEM((tile * 8, lanes), f32),
        ],
        compiler_params=pltpu.CompilerParams(vmem_limit_bytes=24 * 2**20),
        name="finish",
    )(parts, gate, ln_out_gain.reshape(1, channels), w_out)
    return update.reshape(tile, half, channels)


def solution(mesh):
    in_specs = (
        P("row", "col", None),
        P("row", "col"),
        P(),
        P(None, "ch"),
        P(None, "ch"),
        P(None, "ch"),
        P(None, "ch"),
        P(),
        P(),
        P(),
    )
    out_specs = P("row", ("col", "ch"), None)
    return jax.shard_map(shards, mesh=mesh, in_specs=in_specs, out_specs=out_specs, check_vma=False)
```

```python
import jax
import jax.numpy as jnp
from jax import lax
from jax.experimental import pallas as pl
from jax.experimental.pallas import tpu as pltpu
from jax.sharding import PartitionSpec as P

epsilon = 1e-05
f32 = jnp.float32
bf16 = jnp.bfloat16
lanes = 128
chunk = 16


def sigmoid(values):
    return 0.5 * jnp.tanh(0.5 * values) + 0.5


def normalize(values, gain):
    centered = values - jnp.mean(values, axis=-1, keepdims=True)
    spread = jnp.mean(centered * centered, axis=-1, keepdims=True)
    return centered * lax.rsqrt(spread + epsilon) * gain


def project_kernel(
    pair_ref,
    mask_ref,
    gain_ref,
    left_gate_ref,
    left_proj_ref,
    right_gate_ref,
    right_proj_ref,
    message_ref,
    weight_scr,
    normed_scr,
    mask_scr,
    turn_scr,
):
    tile = pair_ref.shape[1]
    part = left_gate_ref.shape[0]

    @pl.when(pl.program_id(0) == 0)
    def _():
        for place, ref in enumerate((left_gate_ref, left_proj_ref, right_gate_ref, right_proj_ref)):
            weight_scr[place * part : (place + 1) * part, :] = ref[...] * 0.5
        normed_scr[...] = jnp.zeros_like(normed_scr)
        mask_scr[...] = jnp.zeros_like(mask_scr)

    normed = normalize(pair_ref[...].astype(f32), gain_ref[...][None])
    normed_scr[:, :tile, :] = normed.astype(bf16)
    mask_scr[:, :tile] = mask_ref[...].astype(f32)

    for k in range(0, chunk, 2):
        source = normed_scr[k : k + 2].reshape(2 * lanes, lanes)
        products = lax.dot_general(
            weight_scr[...], source, (((1,), (1,)), ((), ())), preferred_element_type=f32
        )
        for kk in range(2):
            own_lanes = products[:, kk * lanes : (kk + 1) * lanes]
            valid = mask_scr[k + kk : k + kk + 1, :]
            for side in range(2):
                base = 2 * part * side
                vals = (
                    (jnp.tanh(own_lanes[base : base + part]) + 1.0)
                    * own_lanes[base + part : base + 2 * part]
                    * valid
                )
                turn_scr[side, pl.ds(k + kk, part, stride=chunk), :] = vals
    for side in range(2):
        message_ref[:, side] = turn_scr[side].reshape(part, chunk, lanes).astype(bf16)


def gate_kernel(pair_ref, gain_ref, weight_ref, gate_ref):
    half = pair_ref.shape[1] // 2
    values = pair_ref[...].astype(f32)
    own = jnp.where(lax.axis_index("ch") == 0, values[:, :half], values[:, half:])
    normed = normalize(own, gain_ref[...][None]).reshape(chunk * half, lanes).astype(bf16)
    gate = jnp.dot(normed, weight_ref[...], preferred_element_type=f32)
    gate_ref[...] = sigmoid(gate).reshape(gate_ref.shape)


def product_kernel(left_ref, right_ref, out_ref, right_scr):
    rows, cols = right_ref.shape[0], right_ref.shape[1]
    tile = right_ref.shape[3]
    depth = rows * tile

    @pl.when(pl.program_id(0) == 0)
    def _():
        for q in range(cols):
            block = right_ref[:, q, 0].reshape(depth, lanes)
            right_scr[q * tile : (q + 1) * tile, :] = block.astype(f32).T[:tile].astype(bf16)

    sides = [left_ref[:, p, 0].reshape(depth, lanes) for p in range(left_ref.shape[1])]
    hidden = jnp.dot(
        right_scr[...], jnp.concatenate(sides, axis=1), preferred_element_type=f32
    ).astype(bf16)
    for p in range(left_ref.shape[1]):
        out_ref[p] = hidden[:, p * lanes : (p + 1) * lanes]


def finish_kernel(hidden_ref, gate_ref, gain_ref, weight_ref, out_ref, weight_scr, turn_scr, out_scr):
    channels = hidden_ref.shape[0]
    tile = out_ref.shape[0]

    @pl.when(pl.program_id(0) == 0)
    def _():
        spread_gain = jnp.broadcast_to(gain_ref[...], (channels, channels)).T
        scaled = spread_gain * weight_ref[...].astype(f32)
        part = channels // 2
        for side in range(2):
            turn_scr[pl.ds(side, part, stride=2), :] = scaled[side * part : (side + 1) * part]
        weight_scr[...] = turn_scr[:channels, :].astype(bf16)

    hidden = hidden_ref[:, 0].astype(f32)
    centered = hidden - jnp.mean(hidden, axis=0, keepdims=True)
    spread = jnp.mean(centered * centered, axis=0, keepdims=True)
    normed = centered * lax.rsqrt(spread + epsilon)
    turn_scr[...] = normed.reshape(channels * 8, lanes)
    for j in range(8):
        row = turn_scr[pl.ds(j, channels, stride=8), :].astype(bf16)
        projected = lax.dot_general(
            row, weight_scr[...], (((0,), (0,)), ((), ())), preferred_element_type=f32
        )
        out_scr[pl.ds(j, tile, stride=8), :] = projected[:tile]
    out_ref[:, 0] = (out_scr[...].reshape(tile, 8, lanes) * gate_ref[:, 0]).astype(bf16)


def shards(
    pair,
    pair_mask,
    ln_in_gain,
    w_left_gate,
    w_left_proj,
    w_right_gate,
    w_right_proj,
    w_gate,
    ln_out_gain,
    w_out,
):
    tile, channels = pair.shape[0], pair.shape[2]
    part = w_left_gate.shape[1]
    rows, cols, ch = lax.axis_size("row"), lax.axis_size("col"), lax.axis_size("ch")
    half = tile // ch
    groups = half // 8
    whole = lambda shape: pl.BlockSpec(shape, lambda s: (0,) * len(shape))

    stay = lambda array: pltpu.with_memory_space_constraint(array, pltpu.HBM)
    pair = stay(pair)
    gain_row = stay(ln_in_gain.reshape(1, channels))
    weights = [stay(w.T) for w in (w_left_gate, w_left_proj, w_right_gate, w_right_proj)]
    message = pl.pallas_call(
        project_kernel,
        grid=(tile // chunk,),
        in_specs=[
            pl.BlockSpec((chunk, tile, channels), lambda s: (s, 0, 0)),
            pl.BlockSpec((chunk, tile), lambda s: (s, 0)),
            whole((1, channels)),
            whole((part, channels)),
            whole((part, channels)),
            whole((part, channels)),
            whole((part, channels)),
        ],
        out_specs=pl.BlockSpec((part, 2, chunk, lanes), lambda s: (0, 0, s, 0)),
        out_shape=jax.ShapeDtypeStruct((part, 2, tile, lanes), bf16),
        scratch_shapes=[
            pltpu.VMEM((4 * part, channels), bf16),
            pltpu.VMEM((chunk, lanes, channels), bf16),
            pltpu.VMEM((chunk, lanes), f32),
            pltpu.VMEM((2, part * chunk, lanes), f32),
        ],
        compiler_params=pltpu.CompilerParams(vmem_limit_bytes=24 * 2**20),
        name="project",
    )(pair, stay(pair_mask), gain_row, *weights)

    gate = pl.pallas_call(
        gate_kernel,
        grid=(tile // chunk,),
        in_specs=[
            pl.BlockSpec((chunk, tile, channels), lambda s: (s, 0, 0)),
            whole((1, channels)),
            whole((channels, channels)),
        ],
        out_specs=pl.BlockSpec((chunk, groups, 8, lanes), lambda s: (s, 0, 0, 0)),
        out_shape=jax.ShapeDtypeStruct((tile, groups, 8, lanes), f32),
        compiler_params=pltpu.CompilerParams(vmem_limit_bytes=24 * 2**20),
        cost_estimate=pl.CostEstimate(
            flops=2 * tile * half * channels * channels,
            bytes_accessed=10 * tile * half * channels,
            transcendentals=tile * half * channels,
        ),
        name="gate",
    )(pair, gain_row, stay(w_gate))

    received = lax.all_to_all(message, ("row", "col"), 0, 0, tiled=True)
    received = received.reshape(rows, cols, 2, tile, lanes)

    pairs = 2
    hidden = pl.pallas_call(
        product_kernel,
        grid=(rows // pairs,),
        in_specs=[
            pl.BlockSpec((rows, pairs, 1, tile, lanes), lambda s: (0, s, 0, 0, 0)),
            pl.BlockSpec((rows, cols, 1, tile, lanes), lambda s: (0, 0, 1, 0, 0)),
        ],
        out_specs=pl.BlockSpec((pairs, cols * tile, lanes), lambda s: (s, 0, 0)),
        out_shape=jax.ShapeDtypeStruct((rows, cols * tile, lanes), bf16),
        scratch_shapes=[pltpu.VMEM((cols * tile, rows * tile), bf16)],
        compiler_params=pltpu.CompilerParams(vmem_limit_bytes=24 * 2**20),
        name="product",
    )(received, received)

    parts = lax.all_to_all(
        hidden.reshape(rows * cols * ch, half, lanes), ("row", "col", "ch"), 0, 0, tiled=True
    )
    parts = parts.reshape(channels, groups, 8, lanes)

    update = pl.pallas_call(
        finish_kernel,
        grid=(groups,),
        in_specs=[
            pl.BlockSpec((channels, 1, 8, lanes), lambda s: (0, s, 0, 0)),
            pl.BlockSpec((tile, 1, 8, lanes), lambda s: (0, s, 0, 0)),
            whole((1, channels)),
            whole((channels, channels)),
        ],
        out_specs=pl.BlockSpec((tile, 1, 8, lanes), lambda s: (0, s, 0, 0)),
        out_shape=jax.ShapeDtypeStruct((tile, groups, 8, lanes), bf16),
        scratch_shapes=[
            pltpu.VMEM((channels, channels), bf16),
            pltpu.VMEM((channels * 8, lanes), f32),
            pltpu.VMEM((tile * 8, lanes), f32),
        ],
        compiler_params=pltpu.CompilerParams(vmem_limit_bytes=24 * 2**20),
        name="finish",
    )(parts, gate, stay(ln_out_gain.reshape(1, channels)), stay(w_out))
    return update.reshape(tile, half, channels)


def solution(mesh):
    in_specs = (
        P("row", "col", None),
        P("row", "col"),
        P(),
        P(None, "ch"),
        P(None, "ch"),
        P(None, "ch"),
        P(None, "ch"),
        P(),
        P(),
        P(),
    )
    out_specs = P("row", ("col", "ch"), None)
    return jax.shard_map(shards, mesh=mesh, in_specs=in_specs, out_specs=out_specs, check_vma=False)
```

```python
import jax
import jax.numpy as jnp
from jax import lax
from jax.experimental import pallas as pl
from jax.experimental.pallas import tpu as pltpu
from jax.sharding import PartitionSpec as P

epsilon = 1e-05
f32 = jnp.float32
bf16 = jnp.bfloat16
lanes = 128
chunk = 16
turned = (((1,), (1,)), ((), ()))

edge = 96
spill = 24


def project_kernel(
    pair_hbm,
    mask_ref,
    gain_ref,
    left_gate_ref,
    left_proj_ref,
    right_gate_ref,
    right_proj_ref,
    message_ref,
    pair_scr,
    weight_scr,
    center_scr,
    mask_scr,
    normed_a,
    normed_b,
    upper_a,
    upper_b,
    lower_a,
    lower_b,
    spill_scr,
    sems,
):
    tile = pair_hbm.shape[0]
    part = left_gate_ref.shape[0]
    count = tile // chunk
    order = (count - 1, count - 2) + tuple(range(count - 2))
    normed_refs, uppers, lowers = (normed_a, normed_b), (upper_a, upper_b), (lower_a, lower_b)

    def fetch(c):
        rows = pl.ds(c * chunk, chunk)
        return pltpu.make_async_copy(pair_hbm.at[rows], pair_scr.at[rows], sems.at[c])

    for c in order:
        fetch(c).start()
    gain = gain_ref[...] * 0.5
    for place, ref in enumerate((left_gate_ref, left_proj_ref, right_gate_ref, right_proj_ref)):
        weight_scr[place * part : (place + 1) * part, :] = (ref[...].astype(f32) * gain).astype(bf16)
    rows = lax.broadcasted_iota(jnp.int32, (lanes, lanes), 0)
    cols = lax.broadcasted_iota(jnp.int32, (lanes, lanes), 1)
    center_scr[...] = (jnp.where(rows == cols, 1.0, 0.0) - 1.0 / lanes).astype(bf16)
    mask = mask_ref[...].astype(f32)
    mask_scr[...] = jnp.concatenate([mask, mask[:, edge:]], axis=1)
    lane = lax.broadcasted_iota(jnp.int32, (1, lanes), 1)
    middle = (lane >= edge) & (lane < tile)
    spill_scr[:, 9 * 8 :, :] = jnp.zeros((part, 8, lanes), f32)

    def norm(c, k, normed_ref):
        first, second = pair_scr[c * chunk + k], pair_scr[c * chunk + k + 1]
        source = jnp.concatenate([first, first[edge:], second, second[edge:]], axis=0)
        centered = lax.dot_general(center_scr[...], source, turned, preferred_element_type=f32)
        spread = jnp.sum(centered * centered, axis=0, keepdims=True) * (1.0 / lanes)
        normed_ref[k // 2] = (centered * lax.rsqrt(spread + epsilon)).astype(bf16)

    def values(c, k, normed_ref, upper, lower):
        normed = normed_ref[k // 2]
        left = jnp.dot(weight_scr[: 2 * part], normed, preferred_element_type=f32)
        right = jnp.dot(weight_scr[2 * part :], normed, preferred_element_type=f32)
        for kk in range(2):
            own = slice(kk * lanes, (kk + 1) * lanes)
            row = k + kk
            valid = mask_scr[c * chunk + row : c * chunk + row + 1, :]
            left_vals = (jnp.tanh(left[:part, own]) + 1.0) * left[part:, own] * valid
            right_vals = (jnp.tanh(right[:part, own]) + 1.0) * right[part:, own] * valid
            place = pl.ds(row % 8, part, stride=8)
            upper[row // 8, place, :] = jnp.where(middle, right_vals, left_vals)
            lower[row // 8, place, :] = right_vals

    def store(c, ch, upper, lower):
        def eight(ref, half):
            return ref[half, ch * 8 : (ch + 8) * 8].reshape(8, 8, lanes)

        own = slice(ch, ch + 8)
        at = c * chunk
        message_ref[own, at : at + chunk, :] = jnp.concatenate(
            [eight(upper, 0), eight(upper, 1)], axis=1
        ).astype(bf16)

        def keep(p, half):
            rows = eight(lower, half).reshape(64, lanes)
            for s in range(3):
                to = 8 * (3 * p + s)
                moved = pltpu.roll(rows, edge - 32 * s, 1)
                spill_scr[own, to : to + 8, :] = moved.reshape(8, 8, lanes)

        if c == count - 1:
            keep(1, 0)
            keep(2, 1)
        elif c == count - 2:
            keep(0, 1)
            message_ref[own, tile + at : tile + at + 8, :] = eight(lower, 0).astype(bf16)
        else:
            rows = jnp.concatenate([eight(lower, 0), eight(lower, 1)], axis=1)
            rows = jnp.where(lane[None] < edge, rows, spill_scr[own, at : at + chunk, :])
            message_ref[own, tile + at : tile + at + chunk, :] = rows.astype(bf16)

    for step in range(count + 2):
        if step < count:
            fetch(order[step]).wait()
        for k in range(0, chunk, 2):
            if step < count:
                norm(order[step], k, normed_refs[step % 2])
            if 1 <= step < count + 1:
                last = (step - 1) % 2
                values(order[step - 1], k, normed_refs[last], uppers[last], lowers[last])
            if 2 <= step:
                store(order[step - 2], k * part // chunk, uppers[step % 2], lowers[step % 2])


def normalize(values, gain):
    centered = values - jnp.mean(values, axis=-1, keepdims=True)
    spread = jnp.mean(centered * centered, axis=-1, keepdims=True)
    return centered * lax.rsqrt(spread + epsilon) * gain


def sigmoid(values):
    return 0.5 * jnp.tanh(0.5 * values) + 0.5


def gate_kernel(pair_ref, gain_ref, weight_ref, gate_ref):
    half = pair_ref.shape[1] // 2
    values = pair_ref[...].astype(f32)
    own = jnp.where(lax.axis_index("ch") == 0, values[:, :half], values[:, half:])
    normed = normalize(own, gain_ref[...][None]).reshape(chunk * half, lanes).astype(bf16)
    gate = jnp.dot(normed, weight_ref[...], preferred_element_type=f32)
    gate_ref[...] = sigmoid(gate).reshape(gate_ref.shape)


def product_kernel(received_ref, out_hbm, right_a, right_b, out_scr, sems):
    rows, half_cols, tile = 8, 4, received_ref.shape[1] - 88
    cols, steps = 2 * half_cols, rows // 2
    rights = (right_a, right_b)
    lane = lax.broadcasted_iota(jnp.int32, (1, lanes), 1)

    def turn(q):
        blocks = []
        for r in range(rows):
            upper = received_ref[r * cols + q, :tile].astype(f32)
            lower = received_ref[r * cols + q, tile:].astype(f32)
            parts = [jnp.where(lane < edge, lower, upper[: tile - spill])]
            for p in range(3):
                pieces = [
                    pltpu.roll(lower[8 * (3 * p + s) : 8 * (3 * p + s) + 8], 32 * s + 32, 1)
                    for s in range(3)
                ]
                at = tile - spill + 8 * p
                eight = jnp.where(lane < edge, pieces[2], upper[at : at + 8])
                eight = jnp.where(lane < 64, pieces[1], eight)
                parts.append(jnp.where(lane < 32, pieces[0], eight))
            blocks.append(jnp.concatenate(parts, axis=0).astype(bf16))
        block = jnp.concatenate(blocks, axis=0)
        at = (q % half_cols) * tile
        rights[q // half_cols][at : at + tile, :] = block.T[:tile]

    def send(s, h):
        width = half_cols * tile
        return pltpu.make_async_copy(
            out_scr.at[s, h], out_hbm.at[pl.ds(2 * s, 2), pl.ds(h * width, width)], sems.at[s, h]
        )

    def multiply(s, h):
        lefts = [
            jnp.concatenate([received_ref[r * cols + 2 * s + p, :tile] for r in range(rows)], axis=0)
            for p in range(2)
        ]
        hidden = jnp.dot(
            rights[h][...], jnp.concatenate(lefts, axis=1), preferred_element_type=f32
        ).astype(bf16)
        for p in range(2):
            out_scr[s, h, p] = hidden[:, p * lanes : (p + 1) * lanes]
        send(s, h).start()

    for q in range(half_cols):
        turn(q)
    for s in range(steps):
        turn(half_cols + s)
        multiply(s, 0)
    for s in range(steps):
        multiply(s, 1)
    for s in range(steps):
        for h in range(2):
            send(s, h).wait()


def finish_kernel(
    hidden_hbm,
    gate_hbm,
    gain_ref,
    weight_ref,
    out_hbm,
    hidden_scr,
    gate_scr,
    out_scr,
    weight_scr,
    turn_a,
    turn_b,
    part_a,
    part_b,
    hidden_sems,
    gate_sems,
    out_sems,
):
    groups, channels, tile = hidden_scr.shape[0], hidden_scr.shape[1], out_scr.shape[1]
    turns, outs = (turn_a, turn_b), (part_a, part_b)
    step = 16

    def fetch_hidden(g):
        return pltpu.make_async_copy(hidden_hbm.at[:, g], hidden_scr.at[g], hidden_sems.at[g])

    def fetch_gate(g):
        return pltpu.make_async_copy(gate_hbm.at[:, g], gate_scr.at[g], gate_sems.at[g])

    def send(g):
        return pltpu.make_async_copy(out_scr.at[g], out_hbm.at[:, g], out_sems.at[g])

    for g in range(groups):
        fetch_hidden(g).start()
    for g in range(groups):
        fetch_gate(g).start()
    scaled = jnp.broadcast_to(gain_ref[...], (channels, channels)).T * weight_ref[...].astype(f32)
    part = channels // 2
    for side in range(2):
        turn_a[pl.ds(side, part, stride=2), :] = scaled[side * part : (side + 1) * part]
    weight_scr[...] = turn_a[:channels, :].astype(bf16)

    def tree(terms):
        while len(terms) > 1:
            terms = [terms[n] + terms[n + 1] for n in range(0, len(terms), 2)]
        return terms[0]

    def norm(g):
        def block(c):
            return hidden_scr[g, c : c + step].astype(f32)

        starts = range(0, channels, step)
        center = tree([jnp.sum(block(c), axis=0) for c in starts]) * (1.0 / channels)
        squares = []
        for c in starts:
            centered = block(c) - center[None]
            squares.append(jnp.sum(centered * centered, axis=0))
        scale = lax.rsqrt(tree(squares) * (1.0 / channels) + epsilon)
        for c in starts:
            normed = (block(c) - center[None]) * scale[None]
            turns[g % 2][c * 8 : (c + step) * 8] = normed.reshape(step * 8, lanes)

    def project(g, j):
        row = turns[g % 2][pl.ds(j, channels, stride=8), :].astype(bf16)
        projected = lax.dot_general(
            row, weight_scr[...], (((0,), (0,)), ((), ())), preferred_element_type=f32
        )
        outs[g % 2][pl.ds(j, edge, stride=8), :] = projected[:edge]
        outs[g % 2][pl.ds(edge * 8 + j, tile - edge, stride=8), :] = projected[tile:]

    def multiply(g, n):
        count = tile // 8
        own = slice(n * count, (n + 1) * count)
        rows = outs[g % 2][n * count * 8 : (n + 1) * count * 8].reshape(count, 8, lanes)
        out_scr[g, own] = (rows * gate_scr[g, own]).astype(bf16)

    for s in range(groups + 2):
        if s < groups:
            fetch_hidden(s).wait()
        if 2 <= s:
            fetch_gate(s - 2).wait()
        if s < groups:
            norm(s)
        for j in range(8):
            if 2 <= s:
                multiply(s - 2, j)
            if 1 <= s < groups + 1:
                project(s - 1, j)
        if 2 <= s:
            send(s - 2).start()
    for g in range(groups):
        send(g).wait()


def shards(
    pair,
    pair_mask,
    ln_in_gain,
    w_left_gate,
    w_left_proj,
    w_right_gate,
    w_right_proj,
    w_gate,
    ln_out_gain,
    w_out,
):
    tile, channels = pair.shape[0], pair.shape[2]
    part = w_left_gate.shape[1]
    rows, cols, ch = lax.axis_size("row"), lax.axis_size("col"), lax.axis_size("ch")
    half = tile // ch
    groups = half // 8
    limit = pltpu.CompilerParams(vmem_limit_bytes=24 * 2**20)
    vmem, anywhere = pl.BlockSpec(memory_space=pltpu.VMEM), pl.BlockSpec(memory_space=pl.ANY)
    whole = lambda shape: pl.BlockSpec(shape, lambda s: (0,) * len(shape))

    stay = lambda array: pltpu.with_memory_space_constraint(array, pltpu.HBM)
    pair = stay(pair)
    gain_row = stay(ln_in_gain.reshape(1, channels))
    weights = [stay(w.T) for w in (w_left_gate, w_left_proj, w_right_gate, w_right_proj)]
    normed_shape = pltpu.VMEM((chunk // 2, channels, 2 * lanes), bf16)
    turn_shape = pltpu.VMEM((2, part * 8, lanes), f32)
    message = pl.pallas_call(
        project_kernel,
        in_specs=[anywhere] + [vmem] * 6,
        out_specs=vmem,
        out_shape=jax.ShapeDtypeStruct((part, 2 * tile - spill, lanes), bf16),
        scratch_shapes=[
            pltpu.VMEM(pair.shape, bf16),
            pltpu.VMEM((4 * part, channels), bf16),
            pltpu.VMEM((channels, channels), bf16),
            pltpu.VMEM((tile, lanes), f32),
            normed_shape,
            normed_shape,
            turn_shape,
            turn_shape,
            turn_shape,
            turn_shape,
            pltpu.VMEM((part, 80, lanes), f32),
            pltpu.SemaphoreType.DMA((tile // chunk,)),
        ],
        compiler_params=limit,
        name="project",
    )(pair, stay(pair_mask), gain_row, *weights)

    gate = pl.pallas_call(
        gate_kernel,
        grid=(tile // chunk,),
        in_specs=[
            pl.BlockSpec((chunk, tile, channels), lambda s: (s, 0, 0)),
            whole((1, channels)),
            whole((channels, channels)),
        ],
        out_specs=pl.BlockSpec((chunk, groups, 8, lanes), lambda s: (s, 0, 0, 0)),
        out_shape=jax.ShapeDtypeStruct((tile, groups, 8, lanes), f32),
        compiler_params=limit,
        cost_estimate=pl.CostEstimate(
            flops=2 * tile * half * channels * channels,
            bytes_accessed=10 * tile * half * channels,
            transcendentals=tile * half * channels,
        ),
        name="gate",
    )(pair, gain_row, stay(w_gate))

    received = lax.all_to_all(message, ("row", "col"), 0, 0, tiled=True)

    hidden = pl.pallas_call(
        product_kernel,
        in_specs=[vmem],
        out_specs=anywhere,
        out_shape=jax.ShapeDtypeStruct((rows, cols * tile, lanes), bf16),
        scratch_shapes=[
            pltpu.VMEM((cols * tile // 2, rows * tile), bf16),
            pltpu.VMEM((cols * tile // 2, rows * tile), bf16),
            pltpu.VMEM((rows // 2, 2, 2, cols * tile // 2, lanes), bf16),
            pltpu.SemaphoreType.DMA((rows // 2, 2)),
        ],
        compiler_params=limit,
        name="product",
    )(received)

    parts = lax.all_to_all(
        hidden.reshape(rows * cols * ch, half, lanes), ("row", "col", "ch"), 0, 0, tiled=True
    )
    parts = parts.reshape(channels, groups, 8, lanes)

    update = pl.pallas_call(
        finish_kernel,
        in_specs=[anywhere, anywhere, vmem, vmem],
        out_specs=anywhere,
        out_shape=jax.ShapeDtypeStruct((tile, groups, 8, lanes), bf16),
        scratch_shapes=[
            pltpu.VMEM((groups, channels, 8, lanes), bf16),
            pltpu.VMEM((groups, tile, 8, lanes), f32),
            pltpu.VMEM((groups, tile, 8, lanes), bf16),
            pltpu.VMEM((channels, channels), bf16),
            pltpu.VMEM((channels * 8, lanes), f32),
            pltpu.VMEM((channels * 8, lanes), f32),
            pltpu.VMEM((tile * 8, lanes), f32),
            pltpu.VMEM((tile * 8, lanes), f32),
            pltpu.SemaphoreType.DMA((groups,)),
            pltpu.SemaphoreType.DMA((groups,)),
            pltpu.SemaphoreType.DMA((groups,)),
        ],
        compiler_params=limit,
        name="finish",
    )(parts, gate, ln_out_gain.reshape(1, channels), w_out)
    return update.reshape(tile, half, channels)


def solution(mesh):
    in_specs = (
        P("row", "col", None),
        P("row", "col"),
        P(),
        P(None, "ch"),
        P(None, "ch"),
        P(None, "ch"),
        P(None, "ch"),
        P(),
        P(),
        P(),
    )
    out_specs = P("row", ("col", "ch"), None)
    return jax.shard_map(shards, mesh=mesh, in_specs=in_specs, out_specs=out_specs, check_vma=False)
```

```python
import jax
import jax.numpy as jnp
from jax import lax
from jax.experimental import pallas as pl
from jax.experimental.pallas import tpu as pltpu
from jax.sharding import PartitionSpec as P

epsilon = 1e-05
f32 = jnp.float32
bf16 = jnp.bfloat16
lanes = 128
chunk = 16
turned = (((1,), (1,)), ((), ()))

edge = 96
spill = 24


def project_kernel(
    pair_hbm,
    mask_hbm,
    gain_hbm,
    left_gate_hbm,
    left_proj_hbm,
    right_gate_hbm,
    right_proj_hbm,
    message_ref,
    mask_in,
    gain_in,
    weights_in,
    pair_scr,
    weight_scr,
    center_scr,
    mask_scr,
    normed_a,
    normed_b,
    upper_a,
    upper_b,
    lower_a,
    lower_b,
    spill_scr,
    sems,
    small_sems,
):
    tile = pair_hbm.shape[0]
    part = left_gate_hbm.shape[0]
    count = tile // chunk
    order = (count - 1, count - 2) + tuple(range(count - 2))
    normed_refs, uppers, lowers = (normed_a, normed_b), (upper_a, upper_b), (lower_a, lower_b)

    def fetch(c):
        rows = pl.ds(c * chunk, chunk)
        return pltpu.make_async_copy(pair_hbm.at[rows], pair_scr.at[rows], sems.at[c])

    sources = (left_gate_hbm, left_proj_hbm, right_gate_hbm, right_proj_hbm)
    small = [
        pltpu.make_async_copy(source, weights_in.at[place], small_sems.at[place])
        for place, source in enumerate(sources)
    ]
    small.append(pltpu.make_async_copy(gain_hbm, gain_in, small_sems.at[4]))
    small.append(pltpu.make_async_copy(mask_hbm, mask_in, small_sems.at[5]))
    fetch(order[0]).start()
    for copy in small:
        copy.start()
    for c in order[1:]:
        fetch(c).start()
    rows = lax.broadcasted_iota(jnp.int32, (lanes, lanes), 0)
    cols = lax.broadcasted_iota(jnp.int32, (lanes, lanes), 1)
    center_scr[...] = (jnp.where(rows == cols, 1.0, 0.0) - 1.0 / lanes).astype(bf16)
    lane = lax.broadcasted_iota(jnp.int32, (1, lanes), 1)
    middle = (lane >= edge) & (lane < tile)
    spill_scr[:, 9 * 8 :, :] = jnp.zeros((part, 8, lanes), f32)
    for copy in small:
        copy.wait()
    gain = gain_in[...] * 0.5
    for place in range(4):
        scaled = weights_in[place].astype(f32) * gain
        weight_scr[place * part : (place + 1) * part, :] = scaled.astype(bf16)
    mask = mask_in[...].astype(f32)
    mask_scr[...] = jnp.concatenate([mask, mask[:, edge:]], axis=1)

    def norm(c, k, normed_ref):
        first, second = pair_scr[c * chunk + k], pair_scr[c * chunk + k + 1]
        source = jnp.concatenate([first, first[edge:], second, second[edge:]], axis=0)
        centered = lax.dot_general(center_scr[...], source, turned, preferred_element_type=f32)
        spread = jnp.sum(centered * centered, axis=0, keepdims=True) * (1.0 / lanes)
        normed_ref[k // 2] = (centered * lax.rsqrt(spread + epsilon)).astype(bf16)

    def values(c, k, normed_ref, upper, lower):
        normed = normed_ref[k // 2]
        left = jnp.dot(weight_scr[: 2 * part], normed, preferred_element_type=f32)
        right = jnp.dot(weight_scr[2 * part :], normed, preferred_element_type=f32)
        for kk in range(2):
            own = slice(kk * lanes, (kk + 1) * lanes)
            row = k + kk
            valid = mask_scr[c * chunk + row : c * chunk + row + 1, :]
            left_vals = (jnp.tanh(left[:part, own]) + 1.0) * left[part:, own] * valid
            right_vals = (jnp.tanh(right[:part, own]) + 1.0) * right[part:, own] * valid
            place = pl.ds(row % 8, part, stride=8)
            upper[row // 8, place, :] = jnp.where(middle, right_vals, left_vals)
            lower[row // 8, place, :] = right_vals

    def store(c, ch, upper, lower):
        def eight(ref, half):
            return ref[half, ch * 8 : (ch + 8) * 8].reshape(8, 8, lanes)

        own = slice(ch, ch + 8)
        at = c * chunk
        message_ref[own, at : at + chunk, :] = jnp.concatenate(
            [eight(upper, 0), eight(upper, 1)], axis=1
        ).astype(bf16)

        def keep(p, half):
            rows = eight(lower, half).reshape(64, lanes)
            for s in range(3):
                to = 8 * (3 * p + s)
                moved = pltpu.roll(rows, edge - 32 * s, 1)
                spill_scr[own, to : to + 8, :] = moved.reshape(8, 8, lanes)

        if c == count - 1:
            keep(1, 0)
            keep(2, 1)
        elif c == count - 2:
            keep(0, 1)
            message_ref[own, tile + at : tile + at + 8, :] = eight(lower, 0).astype(bf16)
        else:
            rows = jnp.concatenate([eight(lower, 0), eight(lower, 1)], axis=1)
            rows = jnp.where(lane[None] < edge, rows, spill_scr[own, at : at + chunk, :])
            message_ref[own, tile + at : tile + at + chunk, :] = rows.astype(bf16)

    for step in range(count + 2):
        if step < count:
            fetch(order[step]).wait()
        for k in range(0, chunk, 2):
            if step < count:
                norm(order[step], k, normed_refs[step % 2])
            if 1 <= step < count + 1:
                last = (step - 1) % 2
                values(order[step - 1], k, normed_refs[last], uppers[last], lowers[last])
            if 2 <= step:
                store(order[step - 2], k * part // chunk, uppers[step % 2], lowers[step % 2])


def normalize(values, gain):
    centered = values - jnp.mean(values, axis=-1, keepdims=True)
    spread = jnp.mean(centered * centered, axis=-1, keepdims=True)
    return centered * lax.rsqrt(spread + epsilon) * gain


def sigmoid(values):
    return 0.5 * jnp.tanh(0.5 * values) + 0.5


def gate_kernel(pair_ref, gain_ref, weight_ref, gate_ref):
    half = pair_ref.shape[1] // 2
    values = pair_ref[...].astype(f32)
    own = jnp.where(lax.axis_index("ch") == 0, values[:, :half], values[:, half:])
    normed = normalize(own, gain_ref[...][None]).reshape(chunk * half, lanes).astype(bf16)
    gate = jnp.dot(normed, weight_ref[...], preferred_element_type=f32)
    gate_ref[...] = sigmoid(gate).reshape(gate_ref.shape)


def product_kernel(received_ref, out_hbm, right_a, right_b, out_scr, sems):
    rows, half_cols, tile = 8, 4, received_ref.shape[1] - 88
    cols, steps = 2 * half_cols, rows // 2
    rights = (right_a, right_b)
    lane = lax.broadcasted_iota(jnp.int32, (1, lanes), 1)

    def turn(q):
        blocks = []
        for r in range(rows):
            upper = received_ref[r * cols + q, :tile].astype(f32)
            lower = received_ref[r * cols + q, tile:].astype(f32)
            parts = [jnp.where(lane < edge, lower, upper[: tile - spill])]
            for p in range(3):
                pieces = [
                    pltpu.roll(lower[8 * (3 * p + s) : 8 * (3 * p + s) + 8], 32 * s + 32, 1)
                    for s in range(3)
                ]
                at = tile - spill + 8 * p
                eight = jnp.where(lane < edge, pieces[2], upper[at : at + 8])
                eight = jnp.where(lane < 64, pieces[1], eight)
                parts.append(jnp.where(lane < 32, pieces[0], eight))
            blocks.append(jnp.concatenate(parts, axis=0).astype(bf16))
        block = jnp.concatenate(blocks, axis=0)
        at = (q % half_cols) * tile
        rights[q // half_cols][at : at + tile, :] = block.T[:tile]

    def send(s, h):
        width = half_cols * tile
        return pltpu.make_async_copy(
            out_scr.at[s, h], out_hbm.at[pl.ds(2 * s, 2), pl.ds(h * width, width)], sems.at[s, h]
        )

    def multiply(s, h):
        lefts = [
            jnp.concatenate([received_ref[r * cols + 2 * s + p, :tile] for r in range(rows)], axis=0)
            for p in range(2)
        ]
        hidden = jnp.dot(
            rights[h][...], jnp.concatenate(lefts, axis=1), preferred_element_type=f32
        ).astype(bf16)
        for p in range(2):
            out_scr[s, h, p] = hidden[:, p * lanes : (p + 1) * lanes]
        send(s, h).start()

    for q in range(half_cols):
        turn(q)
    for s in range(steps):
        turn(half_cols + s)
        multiply(s, 0)
    for s in range(steps):
        multiply(s, 1)
    for s in range(steps):
        for h in range(2):
            send(s, h).wait()


def finish_kernel(
    hidden_hbm,
    gate_hbm,
    gain_ref,
    weight_ref,
    out_hbm,
    hidden_scr,
    gate_scr,
    out_scr,
    weight_scr,
    turn_a,
    turn_b,
    part_a,
    part_b,
    center_scr,
    scale_scr,
    hidden_sems,
    gate_sems,
    out_sems,
):
    groups, channels, tile = hidden_scr.shape[0], hidden_scr.shape[1], out_scr.shape[1]
    turns, outs = (turn_a, turn_b), (part_a, part_b)
    step = 16

    def fetch_hidden(g):
        return pltpu.make_async_copy(hidden_hbm.at[:, g], hidden_scr.at[g], hidden_sems.at[g])

    def fetch_gate(g):
        return pltpu.make_async_copy(gate_hbm.at[:, g], gate_scr.at[g], gate_sems.at[g])

    def send(g):
        return pltpu.make_async_copy(out_scr.at[g], out_hbm.at[:, g], out_sems.at[g])

    for g in range(groups):
        fetch_hidden(g).start()
    for g in range(groups):
        fetch_gate(g).start()
    scaled = jnp.broadcast_to(gain_ref[...], (channels, channels)).T * weight_ref[...].astype(f32)
    part = channels // 2
    for side in range(2):
        turn_a[pl.ds(side, part, stride=2), :] = scaled[side * part : (side + 1) * part]
    weight_scr[...] = turn_a[:channels, :].astype(bf16)

    def tree(terms):
        while len(terms) > 1:
            terms = [terms[n] + terms[n + 1] for n in range(0, len(terms), 2)]
        return terms[0]

    def norm(g):
        first = hidden_scr[g, 0].astype(f32)
        sums, squares = [], []
        for c in range(0, channels, step):
            moved = hidden_scr[g, c : c + step].astype(f32) - first[None]
            turns[g % 2][c * 8 : (c + step) * 8] = moved.reshape(step * 8, lanes)
            sums.append(jnp.sum(moved, axis=0))
            squares.append(jnp.sum(moved * moved, axis=0))
        center = tree(sums) * (1.0 / channels)
        spread = tree(squares) * (1.0 / channels) - center * center
        center_scr[g % 2] = center
        scale_scr[g % 2] = lax.rsqrt(jnp.maximum(spread, 0.0) + epsilon)

    def project(g, j):
        moved = turns[g % 2][pl.ds(j, channels, stride=8), :]
        center, scale = center_scr[g % 2, j : j + 1], scale_scr[g % 2, j : j + 1]
        projected = lax.dot_general(
            ((moved - center) * scale).astype(bf16),
            weight_scr[...],
            (((0,), (0,)), ((), ())),
            preferred_element_type=f32,
        )
        outs[g % 2][pl.ds(j, edge, stride=8), :] = projected[:edge]
        outs[g % 2][pl.ds(edge * 8 + j, tile - edge, stride=8), :] = projected[tile:]

    def multiply(g, n):
        count = tile // 8
        own = slice(n * count, (n + 1) * count)
        rows = outs[g % 2][n * count * 8 : (n + 1) * count * 8].reshape(count, 8, lanes)
        out_scr[g, own] = (rows * gate_scr[g, own]).astype(bf16)

    for s in range(groups + 2):
        if s < groups:
            fetch_hidden(s).wait()
        if 2 <= s:
            fetch_gate(s - 2).wait()
        if s < groups:
            norm(s)
        for j in range(8):
            if 2 <= s:
                multiply(s - 2, j)
            if 1 <= s < groups + 1:
                project(s - 1, j)
        if 2 <= s:
            send(s - 2).start()
    for g in range(groups):
        send(g).wait()


def shards(
    pair,
    pair_mask,
    ln_in_gain,
    w_left_gate,
    w_left_proj,
    w_right_gate,
    w_right_proj,
    w_gate,
    ln_out_gain,
    w_out,
):
    tile, channels = pair.shape[0], pair.shape[2]
    part = w_left_gate.shape[1]
    rows, cols, ch = lax.axis_size("row"), lax.axis_size("col"), lax.axis_size("ch")
    half = tile // ch
    groups = half // 8
    limit = pltpu.CompilerParams(vmem_limit_bytes=24 * 2**20)
    vmem, anywhere = pl.BlockSpec(memory_space=pltpu.VMEM), pl.BlockSpec(memory_space=pl.ANY)
    whole = lambda shape: pl.BlockSpec(shape, lambda s: (0,) * len(shape))

    stay = lambda array: pltpu.with_memory_space_constraint(array, pltpu.HBM)
    pair = stay(pair)
    gain_row = stay(ln_in_gain.reshape(1, channels))
    weights = [stay(w.T) for w in (w_left_gate, w_left_proj, w_right_gate, w_right_proj)]
    normed_shape = pltpu.VMEM((chunk // 2, channels, 2 * lanes), bf16)
    turn_shape = pltpu.VMEM((2, part * 8, lanes), f32)
    message = pl.pallas_call(
        project_kernel,
        in_specs=[anywhere] * 7,
        out_specs=vmem,
        out_shape=jax.ShapeDtypeStruct((part, 2 * tile - spill, lanes), bf16),
        scratch_shapes=[
            pltpu.VMEM(pair_mask.shape, jnp.int32),
            pltpu.VMEM((1, channels), f32),
            pltpu.VMEM((4, part, channels), bf16),
            pltpu.VMEM(pair.shape, bf16),
            pltpu.VMEM((4 * part, channels), bf16),
            pltpu.VMEM((channels, channels), bf16),
            pltpu.VMEM((tile, lanes), f32),
            normed_shape,
            normed_shape,
            turn_shape,
            turn_shape,
            turn_shape,
            turn_shape,
            pltpu.VMEM((part, 80, lanes), f32),
            pltpu.SemaphoreType.DMA((tile // chunk,)),
            pltpu.SemaphoreType.DMA((6,)),
        ],
        compiler_params=limit,
        name="project",
    )(pair, stay(pair_mask), gain_row, *weights)

    gate = pl.pallas_call(
        gate_kernel,
        grid=(tile // chunk,),
        in_specs=[
            pl.BlockSpec((chunk, tile, channels), lambda s: (s, 0, 0)),
            whole((1, channels)),
            whole((channels, channels)),
        ],
        out_specs=pl.BlockSpec((chunk, groups, 8, lanes), lambda s: (s, 0, 0, 0)),
        out_shape=jax.ShapeDtypeStruct((tile, groups, 8, lanes), f32),
        compiler_params=limit,
        cost_estimate=pl.CostEstimate(
            flops=2 * tile * half * channels * channels,
            bytes_accessed=10 * tile * half * channels,
            transcendentals=tile * half * channels,
        ),
        name="gate",
    )(pair, gain_row, stay(w_gate))

    received = lax.all_to_all(message, ("row", "col"), 0, 0, tiled=True)

    hidden = pl.pallas_call(
        product_kernel,
        in_specs=[vmem],
        out_specs=anywhere,
        out_shape=jax.ShapeDtypeStruct((rows, cols * tile, lanes), bf16),
        scratch_shapes=[
            pltpu.VMEM((cols * tile // 2, rows * tile), bf16),
            pltpu.VMEM((cols * tile // 2, rows * tile), bf16),
            pltpu.VMEM((rows // 2, 2, 2, cols * tile // 2, lanes), bf16),
            pltpu.SemaphoreType.DMA((rows // 2, 2)),
        ],
        compiler_params=limit,
        name="product",
    )(received)

    parts = lax.all_to_all(
        hidden.reshape(rows * cols * ch, half, lanes), ("row", "col", "ch"), 0, 0, tiled=True
    )
    parts = parts.reshape(channels, groups, 8, lanes)

    update = pl.pallas_call(
        finish_kernel,
        in_specs=[anywhere, anywhere, vmem, vmem],
        out_specs=anywhere,
        out_shape=jax.ShapeDtypeStruct((tile, groups, 8, lanes), bf16),
        scratch_shapes=[
            pltpu.VMEM((groups, channels, 8, lanes), bf16),
            pltpu.VMEM((groups, tile, 8, lanes), f32),
            pltpu.VMEM((groups, tile, 8, lanes), bf16),
            pltpu.VMEM((channels, channels), bf16),
            pltpu.VMEM((channels * 8, lanes), f32),
            pltpu.VMEM((channels * 8, lanes), f32),
            pltpu.VMEM((tile * 8, lanes), f32),
            pltpu.VMEM((tile * 8, lanes), f32),
            pltpu.VMEM((2, 8, lanes), f32),
            pltpu.VMEM((2, 8, lanes), f32),
            pltpu.SemaphoreType.DMA((groups,)),
            pltpu.SemaphoreType.DMA((groups,)),
            pltpu.SemaphoreType.DMA((groups,)),
        ],
        compiler_params=limit,
        name="finish",
    )(parts, gate, ln_out_gain.reshape(1, channels), w_out)
    return update.reshape(tile, half, channels)


def solution(mesh):
    in_specs = (
        P("row", "col", None),
        P("row", "col"),
        P(),
        P(None, "ch"),
        P(None, "ch"),
        P(None, "ch"),
        P(None, "ch"),
        P(),
        P(),
        P(),
    )
    out_specs = P("row", ("col", "ch"), None)
    return jax.shard_map(shards, mesh=mesh, in_specs=in_specs, out_specs=out_specs, check_vma=False)
```

```python
import jax
import jax.numpy as jnp
from jax import lax
from jax.experimental import pallas as pl
from jax.experimental.pallas import tpu as pltpu
from jax.sharding import PartitionSpec as P

epsilon = 1e-05
f32 = jnp.float32
bf16 = jnp.bfloat16
lanes = 128
chunk = 16
turned = (((1,), (1,)), ((), ()))

edge = 96
spill = 24


def project_kernel(
    pair_hbm,
    mask_hbm,
    gain_hbm,
    left_gate_hbm,
    left_proj_hbm,
    right_gate_hbm,
    right_proj_hbm,
    message_ref,
    mask_in,
    gain_in,
    weights_in,
    pair_scr,
    weight_scr,
    center_scr,
    mask_scr,
    normed_a,
    normed_b,
    upper_a,
    upper_b,
    lower_a,
    lower_b,
    spill_scr,
    sems,
    small_sems,
):
    tile = pair_hbm.shape[0]
    part = left_gate_hbm.shape[0]
    count = tile // chunk
    order = (count - 1, count - 2) + tuple(range(count - 2))
    normed_refs, uppers, lowers = (normed_a, normed_b), (upper_a, upper_b), (lower_a, lower_b)

    def fetch(c):
        rows = pl.ds(c * chunk, chunk)
        return pltpu.make_async_copy(pair_hbm.at[rows], pair_scr.at[rows], sems.at[c])

    sources = (left_gate_hbm, left_proj_hbm, right_gate_hbm, right_proj_hbm)
    small = [
        pltpu.make_async_copy(source, weights_in.at[place], small_sems.at[place])
        for place, source in enumerate(sources)
    ]
    small.append(pltpu.make_async_copy(gain_hbm, gain_in, small_sems.at[4]))
    small.append(pltpu.make_async_copy(mask_hbm, mask_in, small_sems.at[5]))
    fetch(order[0]).start()
    for copy in small:
        copy.start()
    fetch(order[1]).start()
    rows = lax.broadcasted_iota(jnp.int32, (lanes, lanes), 0)
    cols = lax.broadcasted_iota(jnp.int32, (lanes, lanes), 1)
    center_scr[...] = (jnp.where(rows == cols, 1.0, 0.0) - 1.0 / lanes).astype(bf16)
    lane = lax.broadcasted_iota(jnp.int32, (1, lanes), 1)
    middle = (lane >= edge) & (lane < tile)
    spill_scr[:, 9 * 8 :, :] = jnp.zeros((part, 8, lanes), f32)
    for copy in small:
        copy.wait()
    gain = gain_in[...] * 0.5
    for place in range(4):
        scaled = weights_in[place].astype(f32) * gain
        weight_scr[place * part : (place + 1) * part, :] = scaled.astype(bf16)
    mask = mask_in[...].astype(f32)
    mask_scr[...] = jnp.concatenate([mask, mask[:, edge:]], axis=1)

    def norm(c, k, normed_ref):
        first, second = pair_scr[c * chunk + k], pair_scr[c * chunk + k + 1]
        source = jnp.concatenate([first, first[edge:], second, second[edge:]], axis=0)
        centered = lax.dot_general(center_scr[...], source, turned, preferred_element_type=f32)
        spread = jnp.sum(centered * centered, axis=0, keepdims=True) * (1.0 / lanes)
        normed_ref[k // 2] = (centered * lax.rsqrt(spread + epsilon)).astype(bf16)

    def values(c, k, normed_ref, upper, lower):
        normed = normed_ref[k // 2]
        left = jnp.dot(weight_scr[: 2 * part], normed, preferred_element_type=f32)
        right = jnp.dot(weight_scr[2 * part :], normed, preferred_element_type=f32)
        for kk in range(2):
            own = slice(kk * lanes, (kk + 1) * lanes)
            row = k + kk
            valid = mask_scr[c * chunk + row : c * chunk + row + 1, :]
            left_vals = (jnp.tanh(left[:part, own]) + 1.0) * left[part:, own] * valid
            right_vals = (jnp.tanh(right[:part, own]) + 1.0) * right[part:, own] * valid
            place = pl.ds(row % 8, part, stride=8)
            upper[row // 8, place, :] = jnp.where(middle, right_vals, left_vals)
            lower[row // 8, place, :] = right_vals

    def store(c, ch, upper, lower):
        def eight(ref, half):
            return ref[half, ch * 8 : (ch + 8) * 8].reshape(8, 8, lanes)

        own = slice(ch, ch + 8)
        at = c * chunk
        message_ref[own, at : at + chunk, :] = jnp.concatenate(
            [eight(upper, 0), eight(upper, 1)], axis=1
        ).astype(bf16)

        def keep(p, half):
            rows = eight(lower, half).reshape(64, lanes)
            for s in range(3):
                to = 8 * (3 * p + s)
                moved = pltpu.roll(rows, edge - 32 * s, 1)
                spill_scr[own, to : to + 8, :] = moved.reshape(8, 8, lanes)

        if c == count - 1:
            keep(1, 0)
            keep(2, 1)
        elif c == count - 2:
            keep(0, 1)
            message_ref[own, tile + at : tile + at + 8, :] = eight(lower, 0).astype(bf16)
        else:
            rows = jnp.concatenate([eight(lower, 0), eight(lower, 1)], axis=1)
            rows = jnp.where(lane[None] < edge, rows, spill_scr[own, at : at + chunk, :])
            message_ref[own, tile + at : tile + at + chunk, :] = rows.astype(bf16)

    for step in range(count + 2):
        if step < count:
            fetch(order[step]).wait()
            if step + 2 < count:
                fetch(order[step + 2]).start()
        for k in range(0, chunk, 2):
            if step < count:
                norm(order[step], k, normed_refs[step % 2])
            if 1 <= step < count + 1:
                last = (step - 1) % 2
                values(order[step - 1], k, normed_refs[last], uppers[last], lowers[last])
            if 2 <= step:
                store(order[step - 2], k * part // chunk, uppers[step % 2], lowers[step % 2])


def normalize(values, gain):
    centered = values - jnp.mean(values, axis=-1, keepdims=True)
    spread = jnp.mean(centered * centered, axis=-1, keepdims=True)
    return centered * lax.rsqrt(spread + epsilon) * gain


def sigmoid(values):
    return 0.5 * jnp.tanh(0.5 * values) + 0.5


def gate_kernel(pair_ref, gain_ref, weight_ref, gate_ref):
    half = pair_ref.shape[1] // 2
    values = pair_ref[...].astype(f32)
    own = jnp.where(lax.axis_index("ch") == 0, values[:, :half], values[:, half:])
    normed = normalize(own, gain_ref[...][None]).reshape(chunk * half, lanes).astype(bf16)
    gate = jnp.dot(normed, weight_ref[...], preferred_element_type=f32)
    gate_ref[...] = sigmoid(gate).reshape(gate_ref.shape)


def product_kernel(received_ref, out_hbm, right_a, right_b, right_c, right_d, out_scr, sems):
    rows, cols, tile = 8, 8, out_hbm.shape[1] // 8
    rights = (right_a, right_b, right_c, right_d)
    blocks_count, steps = len(rights), out_scr.shape[0]
    share, wide = cols // blocks_count, rows // steps
    lane = lax.broadcasted_iota(jnp.int32, (1, lanes), 1)

    def turn(q):
        blocks = []
        for r in range(rows):
            upper = received_ref[r * cols + q, :tile].astype(f32)
            lower = received_ref[r * cols + q, tile:].astype(f32)
            parts = [jnp.where(lane < edge, lower, upper[: tile - spill])]
            for p in range(3):
                pieces = [
                    pltpu.roll(lower[8 * (3 * p + s) : 8 * (3 * p + s) + 8], 32 * s + 32, 1)
                    for s in range(3)
                ]
                at = tile - spill + 8 * p
                eight = jnp.where(lane < edge, pieces[2], upper[at : at + 8])
                eight = jnp.where(lane < 64, pieces[1], eight)
                parts.append(jnp.where(lane < 32, pieces[0], eight))
            blocks.append(jnp.concatenate(parts, axis=0).astype(bf16))
        block = jnp.concatenate(blocks, axis=0)
        at = (q % share) * tile
        rights[q // share][at : at + tile, :] = block.T[:tile]

    def send(s, h):
        width = share * tile
        return pltpu.make_async_copy(
            out_scr.at[s, h],
            out_hbm.at[pl.ds(wide * s, wide), pl.ds(h * width, width)],
            sems.at[s, h],
        )

    def multiply(s, h):
        lefts = [
            jnp.concatenate(
                [received_ref[r * cols + wide * s + p, :tile] for r in range(rows)], axis=0
            )
            for p in range(wide)
        ]
        hidden = jnp.dot(
            rights[h][...], jnp.concatenate(lefts, axis=1), preferred_element_type=f32
        ).astype(bf16)
        for p in range(wide):
            out_scr[s, h, p] = hidden[:, p * lanes : (p + 1) * lanes]
        send(s, h).start()

    for q in range(share):
        turn(q)
    for h in range(blocks_count):
        for s in range(steps):
            if h + 1 < blocks_count:
                turn((h + 1) * share + s)
            multiply(s, h)
    for h in range(blocks_count):
        for s in range(steps):
            send(s, h).wait()


def finish_kernel(
    hidden_hbm,
    gate_hbm,
    gain_ref,
    weight_ref,
    out_hbm,
    hidden_scr,
    gate_scr,
    out_scr,
    weight_scr,
    turn_a,
    turn_b,
    part_a,
    part_b,
    center_scr,
    scale_scr,
    hidden_sems,
    gate_sems,
    out_sems,
):
    groups, channels, tile = hidden_scr.shape[0], hidden_scr.shape[1], out_scr.shape[1]
    turns, outs = (turn_a, turn_b), (part_a, part_b)
    step = 16

    def fetch_hidden(g):
        return pltpu.make_async_copy(hidden_hbm.at[:, g], hidden_scr.at[g], hidden_sems.at[g])

    def fetch_gate(g):
        return pltpu.make_async_copy(gate_hbm.at[:, g], gate_scr.at[g], gate_sems.at[g])

    def send(g):
        return pltpu.make_async_copy(out_scr.at[g], out_hbm.at[:, g], out_sems.at[g])

    for g in range(groups):
        fetch_hidden(g).start()
    for g in range(groups):
        fetch_gate(g).start()
    scaled = jnp.broadcast_to(gain_ref[...], (channels, channels)).T * weight_ref[...].astype(f32)
    part = channels // 2
    for side in range(2):
        turn_a[pl.ds(side, part, stride=2), :] = scaled[side * part : (side + 1) * part]
    weight_scr[...] = turn_a[:channels, :].astype(bf16)

    def tree(terms):
        while len(terms) > 1:
            terms = [terms[n] + terms[n + 1] for n in range(0, len(terms), 2)]
        return terms[0]

    def norm(g):
        first = hidden_scr[g, 0].astype(f32)
        sums, squares = [], []
        for c in range(0, channels, step):
            moved = hidden_scr[g, c : c + step].astype(f32) - first[None]
            turns[g % 2][c * 8 : (c + step) * 8] = moved.reshape(step * 8, lanes)
            sums.append(jnp.sum(moved, axis=0))
            squares.append(jnp.sum(moved * moved, axis=0))
        center = tree(sums) * (1.0 / channels)
        spread = tree(squares) * (1.0 / channels) - center * center
        center_scr[g % 2] = center
        scale_scr[g % 2] = lax.rsqrt(jnp.maximum(spread, 0.0) + epsilon)

    def project(g, j):
        moved = turns[g % 2][pl.ds(j, channels, stride=8), :]
        center, scale = center_scr[g % 2, j : j + 1], scale_scr[g % 2, j : j + 1]
        projected = lax.dot_general(
            ((moved - center) * scale).astype(bf16),
            weight_scr[...],
            (((0,), (0,)), ((), ())),
            preferred_element_type=f32,
        )
        outs[g % 2][pl.ds(j, edge, stride=8), :] = projected[:edge]
        outs[g % 2][pl.ds(edge * 8 + j, tile - edge, stride=8), :] = projected[tile:]

    def multiply(g, n):
        count = tile // 8
        own = slice(n * count, (n + 1) * count)
        rows = outs[g % 2][n * count * 8 : (n + 1) * count * 8].reshape(count, 8, lanes)
        out_scr[g, own] = (rows * gate_scr[g, own]).astype(bf16)

    for s in range(groups + 2):
        if s < groups:
            fetch_hidden(s).wait()
        if 2 <= s:
            fetch_gate(s - 2).wait()
        if s < groups:
            norm(s)
        for j in range(8):
            if 2 <= s:
                multiply(s - 2, j)
            if 1 <= s < groups + 1:
                project(s - 1, j)
        if 2 <= s:
            send(s - 2).start()
    for g in range(groups):
        send(g).wait()


def shards(
    pair,
    pair_mask,
    ln_in_gain,
    w_left_gate,
    w_left_proj,
    w_right_gate,
    w_right_proj,
    w_gate,
    ln_out_gain,
    w_out,
):
    tile, channels = pair.shape[0], pair.shape[2]
    part = w_left_gate.shape[1]
    rows, cols, ch = lax.axis_size("row"), lax.axis_size("col"), lax.axis_size("ch")
    half = tile // ch
    groups = half // 8
    limit = pltpu.CompilerParams(vmem_limit_bytes=24 * 2**20)
    vmem, anywhere = pl.BlockSpec(memory_space=pltpu.VMEM), pl.BlockSpec(memory_space=pl.ANY)
    whole = lambda shape: pl.BlockSpec(shape, lambda s: (0,) * len(shape))

    stay = lambda array: pltpu.with_memory_space_constraint(array, pltpu.HBM)
    pair = stay(pair)
    gain_row = stay(ln_in_gain.reshape(1, channels))
    weights = [stay(w.T) for w in (w_left_gate, w_left_proj, w_right_gate, w_right_proj)]
    normed_shape = pltpu.VMEM((chunk // 2, channels, 2 * lanes), bf16)
    turn_shape = pltpu.VMEM((2, part * 8, lanes), f32)
    message = pl.pallas_call(
        project_kernel,
        in_specs=[anywhere] * 7,
        out_specs=vmem,
        out_shape=jax.ShapeDtypeStruct((part, 2 * tile - spill, lanes), bf16),
        scratch_shapes=[
            pltpu.VMEM(pair_mask.shape, jnp.int32),
            pltpu.VMEM((1, channels), f32),
            pltpu.VMEM((4, part, channels), bf16),
            pltpu.VMEM(pair.shape, bf16),
            pltpu.VMEM((4 * part, channels), bf16),
            pltpu.VMEM((channels, channels), bf16),
            pltpu.VMEM((tile, lanes), f32),
            normed_shape,
            normed_shape,
            turn_shape,
            turn_shape,
            turn_shape,
            turn_shape,
            pltpu.VMEM((part, 80, lanes), f32),
            pltpu.SemaphoreType.DMA((tile // chunk,)),
            pltpu.SemaphoreType.DMA((6,)),
        ],
        compiler_params=limit,
        name="project",
    )(pair, stay(pair_mask), gain_row, *weights)

    gate = pl.pallas_call(
        gate_kernel,
        grid=(tile // chunk,),
        in_specs=[
            pl.BlockSpec((chunk, tile, channels), lambda s: (s, 0, 0)),
            whole((1, channels)),
            whole((channels, channels)),
        ],
        out_specs=pl.BlockSpec((chunk, groups, 8, lanes), lambda s: (s, 0, 0, 0)),
        out_shape=jax.ShapeDtypeStruct((tile, groups, 8, lanes), f32),
        compiler_params=limit,
        cost_estimate=pl.CostEstimate(
            flops=2 * tile * half * channels * channels,
            bytes_accessed=10 * tile * half * channels,
            transcendentals=tile * half * channels,
        ),
        name="gate",
    )(pair, gain_row, stay(w_gate))

    received = lax.all_to_all(message, ("row", "col"), 0, 0, tiled=True)

    right_shape = pltpu.VMEM((cols * tile // 4, rows * tile), bf16)
    hidden = pl.pallas_call(
        product_kernel,
        in_specs=[vmem],
        out_specs=anywhere,
        out_shape=jax.ShapeDtypeStruct((rows, cols * tile, lanes), bf16),
        scratch_shapes=[
            right_shape,
            right_shape,
            right_shape,
            right_shape,
            pltpu.VMEM((2, 4, rows // 2, cols * tile // 4, lanes), bf16),
            pltpu.SemaphoreType.DMA((2, 4)),
        ],
        compiler_params=limit,
        name="product",
    )(received)

    parts = lax.all_to_all(
        hidden.reshape(rows * cols * ch, half, lanes), ("row", "col", "ch"), 0, 0, tiled=True
    )
    parts = parts.reshape(channels, groups, 8, lanes)

    update = pl.pallas_call(
        finish_kernel,
        in_specs=[anywhere, anywhere, vmem, vmem],
        out_specs=anywhere,
        out_shape=jax.ShapeDtypeStruct((tile, groups, 8, lanes), bf16),
        scratch_shapes=[
            pltpu.VMEM((groups, channels, 8, lanes), bf16),
            pltpu.VMEM((groups, tile, 8, lanes), f32),
            pltpu.VMEM((groups, tile, 8, lanes), bf16),
            pltpu.VMEM((channels, channels), bf16),
            pltpu.VMEM((channels * 8, lanes), f32),
            pltpu.VMEM((channels * 8, lanes), f32),
            pltpu.VMEM((tile * 8, lanes), f32),
            pltpu.VMEM((tile * 8, lanes), f32),
            pltpu.VMEM((2, 8, lanes), f32),
            pltpu.VMEM((2, 8, lanes), f32),
            pltpu.SemaphoreType.DMA((groups,)),
            pltpu.SemaphoreType.DMA((groups,)),
            pltpu.SemaphoreType.DMA((groups,)),
        ],
        compiler_params=limit,
        name="finish",
    )(parts, gate, ln_out_gain.reshape(1, channels), w_out)
    return update.reshape(tile, half, channels)


def solution(mesh):
    in_specs = (
        P("row", "col", None),
        P("row", "col"),
        P(),
        P(None, "ch"),
        P(None, "ch"),
        P(None, "ch"),
        P(None, "ch"),
        P(),
        P(),
        P(),
    )
    out_specs = P("row", ("col", "ch"), None)
    return jax.shard_map(shards, mesh=mesh, in_specs=in_specs, out_specs=out_specs, check_vma=False)
```

```python
import jax
import jax.numpy as jnp
from jax import lax
from jax.experimental import pallas as pl
from jax.experimental.pallas import tpu as pltpu
from jax.sharding import PartitionSpec as P

epsilon = 1e-05
f32 = jnp.float32
bf16 = jnp.bfloat16
lanes = 128
chunk = 16
turned = (((1,), (1,)), ((), ()))

edge = 96
spill = 24


def project_kernel(
    pair_hbm,
    mask_hbm,
    gain_hbm,
    left_gate_hbm,
    left_proj_hbm,
    right_gate_hbm,
    right_proj_hbm,
    message_ref,
    mask_in,
    gain_in,
    weights_in,
    pair_scr,
    weight_scr,
    center_scr,
    mask_scr,
    normed_a,
    normed_b,
    upper_a,
    upper_b,
    lower_a,
    lower_b,
    spill_scr,
    sems,
    small_sems,
):
    tile = pair_hbm.shape[0]
    part = left_gate_hbm.shape[0]
    count = tile // chunk
    order = (count - 1, count - 2) + tuple(range(count - 2))
    normed_refs, uppers, lowers = (normed_a, normed_b), (upper_a, upper_b), (lower_a, lower_b)

    def fetch(c):
        rows = pl.ds(c * chunk, chunk)
        return pltpu.make_async_copy(pair_hbm.at[rows], pair_scr.at[rows], sems.at[c])

    sources = (left_gate_hbm, left_proj_hbm, right_gate_hbm, right_proj_hbm)
    small = [
        pltpu.make_async_copy(source, weights_in.at[place], small_sems.at[place])
        for place, source in enumerate(sources)
    ]
    small.append(pltpu.make_async_copy(gain_hbm, gain_in, small_sems.at[4]))
    small.append(pltpu.make_async_copy(mask_hbm, mask_in, small_sems.at[5]))
    fetch(order[0]).start()
    for copy in small:
        copy.start()
    fetch(order[1]).start()
    rows = lax.broadcasted_iota(jnp.int32, (lanes, lanes), 0)
    cols = lax.broadcasted_iota(jnp.int32, (lanes, lanes), 1)
    center_scr[...] = (jnp.where(rows == cols, 1.0, 0.0) - 1.0 / lanes).astype(bf16)
    lane = lax.broadcasted_iota(jnp.int32, (1, lanes), 1)
    middle = (lane >= edge) & (lane < tile)
    spill_scr[:, 9 * 8 :, :] = jnp.zeros((part, 8, lanes), f32)
    for copy in small:
        copy.wait()
    gain = gain_in[...] * 0.5
    for place in range(4):
        scaled = weights_in[place].astype(f32) * gain
        weight_scr[place * part : (place + 1) * part, :] = scaled.astype(bf16)
    mask = mask_in[...].astype(f32)
    mask_scr[...] = jnp.concatenate([mask, mask[:, edge:]], axis=1)

    def norm(c, k, normed_ref):
        first, second = pair_scr[c * chunk + k], pair_scr[c * chunk + k + 1]
        source = jnp.concatenate([first, first[edge:], second, second[edge:]], axis=0)
        centered = lax.dot_general(center_scr[...], source, turned, preferred_element_type=f32)
        spread = jnp.sum(centered * centered, axis=0, keepdims=True) * (1.0 / lanes)
        normed_ref[k // 2] = (centered * lax.rsqrt(spread + epsilon)).astype(bf16)

    def values(c, k, normed_ref, upper, lower):
        normed = normed_ref[k // 2]
        left = jnp.dot(weight_scr[: 2 * part], normed, preferred_element_type=f32)
        right = jnp.dot(weight_scr[2 * part :], normed, preferred_element_type=f32)
        for kk in range(2):
            own = slice(kk * lanes, (kk + 1) * lanes)
            row = k + kk
            valid = mask_scr[c * chunk + row : c * chunk + row + 1, :]
            left_vals = (jnp.tanh(left[:part, own]) + 1.0) * left[part:, own] * valid
            right_vals = (jnp.tanh(right[:part, own]) + 1.0) * right[part:, own] * valid
            place = pl.ds(row % 8, part, stride=8)
            upper[row // 8, place, :] = jnp.where(middle, right_vals, left_vals)
            lower[row // 8, place, :] = right_vals

    def store(c, ch, upper, lower):
        def eight(ref, half):
            return ref[half, ch * 8 : (ch + 8) * 8].reshape(8, 8, lanes)

        own = slice(ch, ch + 8)
        at = c * chunk
        message_ref[own, at : at + chunk, :] = jnp.concatenate(
            [eight(upper, 0), eight(upper, 1)], axis=1
        ).astype(bf16)

        def keep(p, half):
            rows = eight(lower, half).reshape(64, lanes)
            for s in range(3):
                to = 8 * (3 * p + s)
                moved = pltpu.roll(rows, edge - 32 * s, 1)
                spill_scr[own, to : to + 8, :] = moved.reshape(8, 8, lanes)

        if c == count - 1:
            keep(1, 0)
            keep(2, 1)
        elif c == count - 2:
            keep(0, 1)
            message_ref[own, tile + at : tile + at + 8, :] = eight(lower, 0).astype(bf16)
        else:
            rows = jnp.concatenate([eight(lower, 0), eight(lower, 1)], axis=1)
            rows = jnp.where(lane[None] < edge, rows, spill_scr[own, at : at + chunk, :])
            message_ref[own, tile + at : tile + at + chunk, :] = rows.astype(bf16)

    for step in range(count + 2):
        if step == 0:
            fetch(order[0]).wait()
            for c in order[2:]:
                fetch(c).start()
        if step == 1:
            fetch(order[1]).wait()
        if step == 2:
            for c in order[2:]:
                fetch(c).wait()
        for k in range(0, chunk, 2):
            if step < count:
                norm(order[step], k, normed_refs[step % 2])
            if 1 <= step < count + 1:
                last = (step - 1) % 2
                values(order[step - 1], k, normed_refs[last], uppers[last], lowers[last])
            if 2 <= step:
                store(order[step - 2], k * part // chunk, uppers[step % 2], lowers[step % 2])


def normalize(values, gain):
    centered = values - jnp.mean(values, axis=-1, keepdims=True)
    spread = jnp.mean(centered * centered, axis=-1, keepdims=True)
    return centered * lax.rsqrt(spread + epsilon) * gain


def sigmoid(values):
    return 0.5 * jnp.tanh(0.5 * values) + 0.5


def gate_kernel(pair_ref, gain_ref, weight_ref, gate_ref):
    half = pair_ref.shape[1] // 2
    values = pair_ref[...].astype(f32)
    own = jnp.where(lax.axis_index("ch") == 0, values[:, :half], values[:, half:])
    normed = normalize(own, gain_ref[...][None]).reshape(chunk * half, lanes).astype(bf16)
    gate = jnp.dot(normed, weight_ref[...], preferred_element_type=f32)
    gate_ref[...] = sigmoid(gate).reshape(gate_ref.shape)


def product_kernel(received_ref, out_hbm, right_a, right_b, right_c, right_d, out_scr, sems):
    ch, rows, cols, groups = out_hbm.shape[:4]
    tile = ch * groups * 8
    rights = (right_a, right_b, right_c, right_d)
    blocks_count, steps = len(rights), out_scr.shape[0]
    share, wide = cols // blocks_count, rows // steps
    lane = lax.broadcasted_iota(jnp.int32, (1, lanes), 1)

    def turn(q):
        blocks = []
        for r in range(rows):
            upper = received_ref[r * cols + q, :tile].astype(f32)
            lower = received_ref[r * cols + q, tile:].astype(f32)
            parts = [jnp.where(lane < edge, lower, upper[: tile - spill])]
            for p in range(3):
                pieces = [
                    pltpu.roll(lower[8 * (3 * p + s) : 8 * (3 * p + s) + 8], 32 * s + 32, 1)
                    for s in range(3)
                ]
                at = tile - spill + 8 * p
                eight = jnp.where(lane < edge, pieces[2], upper[at : at + 8])
                eight = jnp.where(lane < 64, pieces[1], eight)
                parts.append(jnp.where(lane < 32, pieces[0], eight))
            blocks.append(jnp.concatenate(parts, axis=0).astype(bf16))
        block = jnp.concatenate(blocks, axis=0)
        at = (q % share) * tile
        rights[q // share][at : at + tile, :] = block.T[:tile]

    def send(s, h, side):
        return pltpu.make_async_copy(
            out_scr.at[s, h, side],
            out_hbm.at[side, pl.ds(wide * s, wide), pl.ds(share * h, share)],
            sems.at[s, h, side],
        )

    def multiply(s, h):
        lefts = [
            jnp.concatenate(
                [received_ref[r * cols + wide * s + p, :tile] for r in range(rows)], axis=0
            )
            for p in range(wide)
        ]
        hidden = jnp.dot(
            rights[h][...], jnp.concatenate(lefts, axis=1), preferred_element_type=f32
        )
        for p in range(wide):
            own = hidden[:, p * lanes : (p + 1) * lanes].reshape(share, ch, groups, 8, lanes)
            for side in range(ch):
                out_scr[s, h, side, p] = own[:, side].astype(bf16)
        for side in range(ch):
            send(s, h, side).start()

    for q in range(share):
        turn(q)
    for h in range(blocks_count):
        for s in range(steps):
            if h + 1 < blocks_count:
                turn((h + 1) * share + s)
            multiply(s, h)
    for h in range(blocks_count):
        for s in range(steps):
            for side in range(ch):
                send(s, h, side).wait()


def finish_kernel(
    hidden_hbm,
    gate_ref,
    gain_ref,
    weight_ref,
    out_hbm,
    hidden_scr,
    out_scr,
    weight_scr,
    turn_a,
    turn_b,
    part_a,
    part_b,
    center_scr,
    scale_scr,
    hidden_sems,
    out_sems,
):
    groups, channels, tile = hidden_scr.shape[0], hidden_scr.shape[1], out_scr.shape[1]
    turns, outs = (turn_a, turn_b), (part_a, part_b)
    step = 16

    def fetch_hidden(g):
        return pltpu.make_async_copy(hidden_hbm.at[:, g], hidden_scr.at[g], hidden_sems.at[g])

    def send(g):
        return pltpu.make_async_copy(out_scr.at[g], out_hbm.at[:, g], out_sems.at[g])

    for g in range(groups):
        fetch_hidden(g).start()
    scaled = jnp.broadcast_to(gain_ref[...], (channels, channels)).T * weight_ref[...].astype(f32)
    weight_scr[...] = scaled.astype(bf16)

    def tree(terms):
        while len(terms) > 1:
            terms = [terms[n] + terms[n + 1] for n in range(0, len(terms), 2)]
        return terms[0]

    def norm(g):
        first = hidden_scr[g, 0].astype(f32)
        sums, squares = [], []
        for c in range(0, channels, step):
            moved = hidden_scr[g, c : c + step].astype(f32) - first[None]
            turns[g % 2][c * 8 : (c + step) * 8] = moved.reshape(step * 8, lanes)
            sums.append(jnp.sum(moved, axis=0))
            squares.append(jnp.sum(moved * moved, axis=0))
        center = tree(sums) * (1.0 / channels)
        spread = tree(squares) * (1.0 / channels) - center * center
        center_scr[g % 2] = center
        scale_scr[g % 2] = lax.rsqrt(jnp.maximum(spread, 0.0) + epsilon)

    def project(g, j):
        moved = turns[g % 2][pl.ds(j, channels, stride=8), :]
        center, scale = center_scr[g % 2, j : j + 1], scale_scr[g % 2, j : j + 1]
        projected = lax.dot_general(
            ((moved - center) * scale).astype(bf16),
            weight_scr[...],
            (((0,), (0,)), ((), ())),
            preferred_element_type=f32,
        )
        outs[g % 2][pl.ds(j, edge, stride=8), :] = projected[:edge]
        outs[g % 2][pl.ds(edge * 8 + j, tile - edge, stride=8), :] = projected[tile:]

    def multiply(g, n):
        count = tile // 8
        own = slice(n * count, (n + 1) * count)
        rows = outs[g % 2][n * count * 8 : (n + 1) * count * 8].reshape(count, 8, lanes)
        out_scr[g, own] = (rows * gate_ref[own, g]).astype(bf16)

    arrivals = {0: (0,), 1: (1, 2), 3: tuple(range(3, groups))}
    for s in range(groups + 2):
        for g in arrivals.get(s, ()):
            fetch_hidden(g).wait()
        if s < groups:
            norm(s)
        for j in range(8):
            if 2 <= s:
                multiply(s - 2, j)
            if 1 <= s < groups + 1:
                project(s - 1, j)
        if 2 <= s:
            send(s - 2).start()
    for g in range(groups):
        send(g).wait()


def shards(
    pair,
    pair_mask,
    ln_in_gain,
    w_left_gate,
    w_left_proj,
    w_right_gate,
    w_right_proj,
    w_gate,
    ln_out_gain,
    w_out,
):
    tile, channels = pair.shape[0], pair.shape[2]
    part = w_left_gate.shape[1]
    rows, cols, ch = lax.axis_size("row"), lax.axis_size("col"), lax.axis_size("ch")
    half = tile // ch
    groups = half // 8
    limit = pltpu.CompilerParams(vmem_limit_bytes=24 * 2**20)
    vmem, anywhere = pl.BlockSpec(memory_space=pltpu.VMEM), pl.BlockSpec(memory_space=pl.ANY)
    whole = lambda shape: pl.BlockSpec(shape, lambda s: (0,) * len(shape))

    stay = lambda array: pltpu.with_memory_space_constraint(array, pltpu.HBM)
    pair = stay(pair)
    gain_row = stay(ln_in_gain.reshape(1, channels))
    weights = [stay(w.T) for w in (w_left_gate, w_left_proj, w_right_gate, w_right_proj)]
    normed_shape = pltpu.VMEM((chunk // 2, channels, 2 * lanes), bf16)
    turn_shape = pltpu.VMEM((2, part * 8, lanes), f32)
    message = pl.pallas_call(
        project_kernel,
        in_specs=[anywhere] * 7,
        out_specs=vmem,
        out_shape=jax.ShapeDtypeStruct((part, 2 * tile - spill, lanes), bf16),
        scratch_shapes=[
            pltpu.VMEM(pair_mask.shape, jnp.int32),
            pltpu.VMEM((1, channels), f32),
            pltpu.VMEM((4, part, channels), bf16),
            pltpu.VMEM(pair.shape, bf16),
            pltpu.VMEM((4 * part, channels), bf16),
            pltpu.VMEM((channels, channels), bf16),
            pltpu.VMEM((tile, lanes), f32),
            normed_shape,
            normed_shape,
            turn_shape,
            turn_shape,
            turn_shape,
            turn_shape,
            pltpu.VMEM((part, 80, lanes), f32),
            pltpu.SemaphoreType.DMA((tile // chunk,)),
            pltpu.SemaphoreType.DMA((6,)),
        ],
        compiler_params=limit,
        name="project",
    )(pair, stay(pair_mask), gain_row, *weights)

    gate = pl.pallas_call(
        gate_kernel,
        grid=(tile // chunk,),
        in_specs=[
            pl.BlockSpec((chunk, tile, channels), lambda s: (s, 0, 0)),
            whole((1, channels)),
            whole((channels, channels)),
        ],
        out_specs=pl.BlockSpec((chunk, groups, 8, lanes), lambda s: (s, 0, 0, 0)),
        out_shape=jax.ShapeDtypeStruct((tile, groups, 8, lanes), f32),
        compiler_params=limit,
        cost_estimate=pl.CostEstimate(
            flops=2 * tile * half * channels * channels,
            bytes_accessed=10 * tile * half * channels,
            transcendentals=tile * half * channels,
        ),
        name="gate",
    )(pair, gain_row, stay(w_gate))

    received = lax.all_to_all(message, ("row", "col"), 0, 0, tiled=True)

    right_shape = pltpu.VMEM((cols * tile // 4, rows * tile), bf16)
    hidden = pl.pallas_call(
        product_kernel,
        in_specs=[vmem],
        out_specs=anywhere,
        out_shape=jax.ShapeDtypeStruct((ch, rows, cols, groups, 8, lanes), bf16),
        scratch_shapes=[
            right_shape,
            right_shape,
            right_shape,
            right_shape,
            pltpu.VMEM((2, 4, ch, rows // 2, cols // 4, groups, 8, lanes), bf16),
            pltpu.SemaphoreType.DMA((2, 4, ch)),
        ],
        compiler_params=limit,
        name="product",
    )(received)

    parts = lax.all_to_all(
        hidden.reshape(channels, groups, 8, lanes), ("ch", "row", "col"), 0, 0, tiled=True
    )

    update = pl.pallas_call(
        finish_kernel,
        in_specs=[anywhere, vmem, vmem, vmem],
        out_specs=anywhere,
        out_shape=jax.ShapeDtypeStruct((tile, groups, 8, lanes), bf16),
        scratch_shapes=[
            pltpu.VMEM((groups, channels, 8, lanes), bf16),
            pltpu.VMEM((groups, tile, 8, lanes), bf16),
            pltpu.VMEM((channels, channels), bf16),
            pltpu.VMEM((channels * 8, lanes), f32),
            pltpu.VMEM((channels * 8, lanes), f32),
            pltpu.VMEM((tile * 8, lanes), f32),
            pltpu.VMEM((tile * 8, lanes), f32),
            pltpu.VMEM((2, 8, lanes), f32),
            pltpu.VMEM((2, 8, lanes), f32),
            pltpu.SemaphoreType.DMA((groups,)),
            pltpu.SemaphoreType.DMA((groups,)),
        ],
        compiler_params=limit,
        name="finish",
    )(parts, gate, ln_out_gain.reshape(1, channels), w_out)
    return update.reshape(tile, half, channels)


def solution(mesh):
    in_specs = (
        P("row", "col", None),
        P("row", "col"),
        P(),
        P(None, "ch"),
        P(None, "ch"),
        P(None, "ch"),
        P(None, "ch"),
        P(),
        P(),
        P(),
    )
    out_specs = P("row", ("col", "ch"), None)
    return jax.shard_map(shards, mesh=mesh, in_specs=in_specs, out_specs=out_specs, check_vma=False)
```

```python
import jax
import jax.numpy as jnp
from jax import lax
from jax.experimental import pallas as pl
from jax.experimental.pallas import tpu as pltpu
from jax.sharding import PartitionSpec as P

epsilon = 1e-05
f32 = jnp.float32
bf16 = jnp.bfloat16
lanes = 128
chunk = 16
turned = (((1,), (1,)), ((), ()))

edge = 96
spill = 24


def project_kernel(
    pair_hbm,
    mask_hbm,
    gain_hbm,
    left_gate_hbm,
    left_proj_hbm,
    right_gate_hbm,
    right_proj_hbm,
    message_ref,
    mask_in,
    gain_in,
    weights_in,
    pair_scr,
    weight_scr,
    center_scr,
    mask_scr,
    normed_a,
    normed_b,
    upper_a,
    upper_b,
    lower_a,
    lower_b,
    spill_scr,
    sems,
    small_sems,
):
    tile = pair_hbm.shape[0]
    part = left_gate_hbm.shape[0]
    count = tile // chunk
    order = (count - 1, count - 2) + tuple(range(count - 2))
    normed_refs, uppers, lowers = (normed_a, normed_b), (upper_a, upper_b), (lower_a, lower_b)

    def fetch(c):
        rows = pl.ds(c * chunk, chunk)
        return pltpu.make_async_copy(pair_hbm.at[rows], pair_scr.at[rows], sems.at[c])

    sources = (left_gate_hbm, left_proj_hbm, right_gate_hbm, right_proj_hbm)
    small = [
        pltpu.make_async_copy(source, weights_in.at[place], small_sems.at[place])
        for place, source in enumerate(sources)
    ]
    small.append(pltpu.make_async_copy(gain_hbm, gain_in, small_sems.at[4]))
    small.append(pltpu.make_async_copy(mask_hbm, mask_in, small_sems.at[5]))
    fetch(order[0]).start()
    for copy in small:
        copy.start()
    fetch(order[1]).start()
    rows = lax.broadcasted_iota(jnp.int32, (lanes, lanes), 0)
    cols = lax.broadcasted_iota(jnp.int32, (lanes, lanes), 1)
    center_scr[...] = (jnp.where(rows == cols, 1.0, 0.0) - 1.0 / lanes).astype(bf16)
    lane = lax.broadcasted_iota(jnp.int32, (1, lanes), 1)
    middle = (lane >= edge) & (lane < tile)
    spill_scr[:, 9 * 8 :, :] = jnp.zeros((part, 8, lanes), f32)
    for copy in small:
        copy.wait()
    gain = gain_in[...] * 0.5
    for place in range(4):
        scaled = weights_in[place].astype(f32) * gain
        weight_scr[place * part : (place + 1) * part, :] = scaled.astype(bf16)
    mask = mask_in[...].astype(f32)
    mask_scr[...] = jnp.concatenate([mask, mask[:, edge:]], axis=1)

    def norm(c, k, normed_ref):
        first, second = pair_scr[c * chunk + k], pair_scr[c * chunk + k + 1]
        source = jnp.concatenate([first, first[edge:], second, second[edge:]], axis=0)
        centered = lax.dot_general(center_scr[...], source, turned, preferred_element_type=f32)
        spread = jnp.sum(centered * centered, axis=0, keepdims=True) * (1.0 / lanes)
        at = c * chunk + k
        valid = jnp.concatenate([mask_scr[at : at + 1, :], mask_scr[at + 1 : at + 2, :]], axis=1)
        normed_ref[k // 2] = (centered * (lax.rsqrt(spread + epsilon) * valid)).astype(bf16)

    def values(k, normed_ref, upper, lower):
        normed = normed_ref[k // 2]
        left = jnp.dot(weight_scr[: 2 * part], normed, preferred_element_type=f32)
        right = jnp.dot(weight_scr[2 * part :], normed, preferred_element_type=f32)
        for kk in range(2):
            own = slice(kk * lanes, (kk + 1) * lanes)
            row = k + kk
            left_vals = (jnp.tanh(left[:part, own]) + 1.0) * left[part:, own]
            right_vals = (jnp.tanh(right[:part, own]) + 1.0) * right[part:, own]
            place = pl.ds(row % 8, part, stride=8)
            upper[row // 8, place, :] = jnp.where(middle, right_vals, left_vals)
            lower[row // 8, place, :] = right_vals

    def store(c, ch, upper, lower):
        def eight(ref, half):
            return ref[half, ch * 8 : (ch + 8) * 8].reshape(8, 8, lanes)

        own = slice(ch, ch + 8)
        at = c * chunk
        message_ref[own, at : at + chunk, :] = jnp.concatenate(
            [eight(upper, 0), eight(upper, 1)], axis=1
        ).astype(bf16)

        def keep(p, half):
            rows = eight(lower, half).reshape(64, lanes)
            for s in range(3):
                to = 8 * (3 * p + s)
                moved = pltpu.roll(rows, edge - 32 * s, 1)
                spill_scr[own, to : to + 8, :] = moved.reshape(8, 8, lanes)

        if c == count - 1:
            keep(1, 0)
            keep(2, 1)
        elif c == count - 2:
            keep(0, 1)
            message_ref[own, tile + at : tile + at + 8, :] = eight(lower, 0).astype(bf16)
        else:
            rows = jnp.concatenate([eight(lower, 0), eight(lower, 1)], axis=1)
            rows = jnp.where(lane[None] < edge, rows, spill_scr[own, at : at + chunk, :])
            message_ref[own, tile + at : tile + at + chunk, :] = rows.astype(bf16)

    for step in range(count + 2):
        if step == 0:
            fetch(order[0]).wait()
            for c in order[2:]:
                fetch(c).start()
        if step == 1:
            fetch(order[1]).wait()
        if step == 2:
            for c in order[2:]:
                fetch(c).wait()
        for k in range(0, chunk, 2):
            if step < count:
                norm(order[step], k, normed_refs[step % 2])
            if 1 <= step < count + 1:
                last = (step - 1) % 2
                values(k, normed_refs[last], uppers[last], lowers[last])
            if 2 <= step:
                store(order[step - 2], k * part // chunk, uppers[step % 2], lowers[step % 2])


def normalize(values, gain):
    centered = values - jnp.mean(values, axis=-1, keepdims=True)
    spread = jnp.mean(centered * centered, axis=-1, keepdims=True)
    return centered * lax.rsqrt(spread + epsilon) * gain


def sigmoid(values):
    return 0.5 * jnp.tanh(0.5 * values) + 0.5


def gate_kernel(pair_ref, gain_ref, weight_ref, gate_ref):
    half = pair_ref.shape[1] // 2
    values = pair_ref[...].astype(f32)
    own = jnp.where(lax.axis_index("ch") == 0, values[:, :half], values[:, half:])
    normed = normalize(own, gain_ref[...][None]).reshape(chunk * half, lanes).astype(bf16)
    gate = jnp.dot(normed, weight_ref[...], preferred_element_type=f32)
    gate_ref[...] = sigmoid(gate).reshape(gate_ref.shape)


def product_kernel(received_ref, out_hbm, right_a, right_b, right_c, right_d, out_scr, sems):
    ch, rows, cols, groups = out_hbm.shape[:4]
    tile = ch * groups * 8
    rights = (right_a, right_b, right_c, right_d)
    blocks_count, steps = len(rights), out_scr.shape[0]
    share, wide = cols // blocks_count, rows // steps
    lane = lax.broadcasted_iota(jnp.int32, (1, lanes), 1)

    def turn(q):
        blocks = []
        for r in range(rows):
            upper = received_ref[r * cols + q, :tile].astype(f32)
            lower = received_ref[r * cols + q, tile:].astype(f32)
            parts = [jnp.where(lane < edge, lower, upper[: tile - spill])]
            for p in range(3):
                pieces = [
                    pltpu.roll(lower[8 * (3 * p + s) : 8 * (3 * p + s) + 8], 32 * s + 32, 1)
                    for s in range(3)
                ]
                at = tile - spill + 8 * p
                eight = jnp.where(lane < edge, pieces[2], upper[at : at + 8])
                eight = jnp.where(lane < 64, pieces[1], eight)
                parts.append(jnp.where(lane < 32, pieces[0], eight))
            blocks.append(jnp.concatenate(parts, axis=0).astype(bf16))
        block = jnp.concatenate(blocks, axis=0)
        at = (q % share) * tile
        rights[q // share][at : at + tile, :] = block.T[:tile]

    def send(s, h, side):
        return pltpu.make_async_copy(
            out_scr.at[s, h, side],
            out_hbm.at[side, pl.ds(wide * s, wide), pl.ds(share * h, share)],
            sems.at[s, h, side],
        )

    def multiply(s, h):
        lefts = [
            jnp.concatenate(
                [received_ref[r * cols + wide * s + p, :tile] for r in range(rows)], axis=0
            )
            for p in range(wide)
        ]
        hidden = jnp.dot(
            rights[h][...], jnp.concatenate(lefts, axis=1), preferred_element_type=f32
        )
        for p in range(wide):
            own = hidden[:, p * lanes : (p + 1) * lanes].reshape(share, ch, groups, 8, lanes)
            for side in range(ch):
                out_scr[s, h, side, p] = own[:, side].astype(bf16)
        for side in range(ch):
            send(s, h, side).start()

    for q in range(share):
        turn(q)
    for h in range(blocks_count):
        for s in range(steps):
            if h + 1 < blocks_count:
                turn((h + 1) * share + s)
            multiply(s, h)
    for h in range(blocks_count):
        for s in range(steps):
            for side in range(ch):
                send(s, h, side).wait()


def finish_kernel(
    hidden_hbm,
    gate_ref,
    gain_ref,
    weight_ref,
    out_hbm,
    hidden_scr,
    out_scr,
    weight_scr,
    turn_a,
    turn_b,
    part_a,
    part_b,
    center_scr,
    scale_scr,
    hidden_sems,
    out_sems,
):
    groups, channels, tile = hidden_scr.shape[0], hidden_scr.shape[1], out_scr.shape[1]
    turns, outs = (turn_a, turn_b), (part_a, part_b)
    step = 16

    def fetch_hidden(g):
        return pltpu.make_async_copy(hidden_hbm.at[:, g], hidden_scr.at[g], hidden_sems.at[g])

    def send(g):
        return pltpu.make_async_copy(out_scr.at[g], out_hbm.at[:, g], out_sems.at[g])

    for g in range(groups):
        fetch_hidden(g).start()
    scaled = jnp.broadcast_to(gain_ref[...], (channels, channels)).T * weight_ref[...].astype(f32)
    weight_scr[...] = scaled.astype(bf16)

    def tree(terms):
        while len(terms) > 1:
            terms = [terms[n] + terms[n + 1] for n in range(0, len(terms), 2)]
        return terms[0]

    def norm(g):
        first = hidden_scr[g, 0].astype(f32)
        sums, squares = [], []
        for c in range(0, channels, step):
            moved = hidden_scr[g, c : c + step].astype(f32) - first[None]
            turns[g % 2][c * 8 : (c + step) * 8] = moved.reshape(step * 8, lanes)
            sums.append(jnp.sum(moved, axis=0))
            squares.append(jnp.sum(moved * moved, axis=0))
        center = tree(sums) * (1.0 / channels)
        spread = tree(squares) * (1.0 / channels) - center * center
        center_scr[g % 2] = center
        scale_scr[g % 2] = lax.rsqrt(jnp.maximum(spread, 0.0) + epsilon)

    def project(g, j):
        moved = turns[g % 2][pl.ds(j, channels, stride=8), :]
        center, scale = center_scr[g % 2, j : j + 1], scale_scr[g % 2, j : j + 1]
        projected = lax.dot_general(
            ((moved - center) * scale).astype(bf16),
            weight_scr[...],
            (((0,), (0,)), ((), ())),
            preferred_element_type=f32,
        )
        outs[g % 2][pl.ds(j, edge, stride=8), :] = projected[:edge]
        outs[g % 2][pl.ds(edge * 8 + j, tile - edge, stride=8), :] = projected[tile:]

    def multiply(g, n):
        count = tile // 8
        own = slice(n * count, (n + 1) * count)
        rows = outs[g % 2][n * count * 8 : (n + 1) * count * 8].reshape(count, 8, lanes)
        out_scr[g, own] = (rows * gate_ref[own, g]).astype(bf16)

    arrivals = {0: (0,), 1: (1, 2), 3: tuple(range(3, groups))}
    for s in range(groups + 2):
        for g in arrivals.get(s, ()):
            fetch_hidden(g).wait()
        if s < groups:
            norm(s)
        for j in range(8):
            if 2 <= s:
                multiply(s - 2, j)
            if 1 <= s < groups + 1:
                project(s - 1, j)
        if 2 <= s:
            send(s - 2).start()
    for g in range(groups):
        send(g).wait()


def shards(
    pair,
    pair_mask,
    ln_in_gain,
    w_left_gate,
    w_left_proj,
    w_right_gate,
    w_right_proj,
    w_gate,
    ln_out_gain,
    w_out,
):
    tile, channels = pair.shape[0], pair.shape[2]
    part = w_left_gate.shape[1]
    rows, cols, ch = lax.axis_size("row"), lax.axis_size("col"), lax.axis_size("ch")
    half = tile // ch
    groups = half // 8
    limit = pltpu.CompilerParams(vmem_limit_bytes=24 * 2**20)
    vmem, anywhere = pl.BlockSpec(memory_space=pltpu.VMEM), pl.BlockSpec(memory_space=pl.ANY)
    whole = lambda shape: pl.BlockSpec(shape, lambda s: (0,) * len(shape))

    stay = lambda array: pltpu.with_memory_space_constraint(array, pltpu.HBM)
    pair = stay(pair)
    gain_row = stay(ln_in_gain.reshape(1, channels))
    weights = [stay(w.T) for w in (w_left_gate, w_left_proj, w_right_gate, w_right_proj)]
    normed_shape = pltpu.VMEM((chunk // 2, channels, 2 * lanes), bf16)
    turn_shape = pltpu.VMEM((2, part * 8, lanes), f32)
    message = pl.pallas_call(
        project_kernel,
        in_specs=[anywhere] * 7,
        out_specs=vmem,
        out_shape=jax.ShapeDtypeStruct((part, 2 * tile - spill, lanes), bf16),
        scratch_shapes=[
            pltpu.VMEM(pair_mask.shape, jnp.int32),
            pltpu.VMEM((1, channels), f32),
            pltpu.VMEM((4, part, channels), bf16),
            pltpu.VMEM(pair.shape, bf16),
            pltpu.VMEM((4 * part, channels), bf16),
            pltpu.VMEM((channels, channels), bf16),
            pltpu.VMEM((tile, lanes), f32),
            normed_shape,
            normed_shape,
            turn_shape,
            turn_shape,
            turn_shape,
            turn_shape,
            pltpu.VMEM((part, 80, lanes), f32),
            pltpu.SemaphoreType.DMA((tile // chunk,)),
            pltpu.SemaphoreType.DMA((6,)),
        ],
        compiler_params=limit,
        name="project",
    )(pair, stay(pair_mask), gain_row, *weights)

    gate = pl.pallas_call(
        gate_kernel,
        grid=(tile // chunk,),
        in_specs=[
            pl.BlockSpec((chunk, tile, channels), lambda s: (s, 0, 0)),
            whole((1, channels)),
            whole((channels, channels)),
        ],
        out_specs=pl.BlockSpec((chunk, groups, 8, lanes), lambda s: (s, 0, 0, 0)),
        out_shape=jax.ShapeDtypeStruct((tile, groups, 8, lanes), f32),
        compiler_params=limit,
        cost_estimate=pl.CostEstimate(
            flops=2 * tile * half * channels * channels,
            bytes_accessed=10 * tile * half * channels,
            transcendentals=tile * half * channels,
        ),
        name="gate",
    )(pair, gain_row, stay(w_gate))

    received = lax.all_to_all(message, ("row", "col"), 0, 0, tiled=True)

    right_shape = pltpu.VMEM((cols * tile // 4, rows * tile), bf16)
    hidden = pl.pallas_call(
        product_kernel,
        in_specs=[vmem],
        out_specs=anywhere,
        out_shape=jax.ShapeDtypeStruct((ch, rows, cols, groups, 8, lanes), bf16),
        scratch_shapes=[
            right_shape,
            right_shape,
            right_shape,
            right_shape,
            pltpu.VMEM((2, 4, ch, rows // 2, cols // 4, groups, 8, lanes), bf16),
            pltpu.SemaphoreType.DMA((2, 4, ch)),
        ],
        compiler_params=limit,
        name="product",
    )(received)

    parts = lax.all_to_all(
        hidden.reshape(channels, groups, 8, lanes), ("ch", "row", "col"), 0, 0, tiled=True
    )

    update = pl.pallas_call(
        finish_kernel,
        in_specs=[anywhere, vmem, vmem, vmem],
        out_specs=anywhere,
        out_shape=jax.ShapeDtypeStruct((tile, groups, 8, lanes), bf16),
        scratch_shapes=[
            pltpu.VMEM((groups, channels, 8, lanes), bf16),
            pltpu.VMEM((groups, tile, 8, lanes), bf16),
            pltpu.VMEM((channels, channels), bf16),
            pltpu.VMEM((channels * 8, lanes), f32),
            pltpu.VMEM((channels * 8, lanes), f32),
            pltpu.VMEM((tile * 8, lanes), f32),
            pltpu.VMEM((tile * 8, lanes), f32),
            pltpu.VMEM((2, 8, lanes), f32),
            pltpu.VMEM((2, 8, lanes), f32),
            pltpu.SemaphoreType.DMA((groups,)),
            pltpu.SemaphoreType.DMA((groups,)),
        ],
        compiler_params=limit,
        name="finish",
    )(parts, gate, ln_out_gain.reshape(1, channels), w_out)
    return update.reshape(tile, half, channels)


def solution(mesh):
    in_specs = (
        P("row", "col", None),
        P("row", "col"),
        P(),
        P(None, "ch"),
        P(None, "ch"),
        P(None, "ch"),
        P(None, "ch"),
        P(),
        P(),
        P(),
    )
    out_specs = P("row", ("col", "ch"), None)
    return jax.shard_map(shards, mesh=mesh, in_specs=in_specs, out_specs=out_specs, check_vma=False)
```

```python
import jax
import jax.numpy as jnp
from jax import lax
from jax.experimental import pallas as pl
from jax.experimental.pallas import tpu as pltpu
from jax.sharding import PartitionSpec as P

epsilon = 1e-05
f32 = jnp.float32
bf16 = jnp.bfloat16
lanes = 128
chunk = 16
turned = (((1,), (1,)), ((), ()))

edge = 96
spill = 24


def project_kernel(
    pair_hbm,
    mask_hbm,
    gain_hbm,
    left_gate_hbm,
    left_proj_hbm,
    right_gate_hbm,
    right_proj_hbm,
    message_ref,
    mask_in,
    gain_in,
    weights_in,
    pair_scr,
    weight_scr,
    center_scr,
    mask_scr,
    normed_a,
    normed_b,
    upper_a,
    upper_b,
    lower_a,
    lower_b,
    spill_scr,
    sems,
    small_sems,
):
    tile = pair_hbm.shape[0]
    part = left_gate_hbm.shape[0]
    count = tile // chunk
    order = (count - 1, count - 2) + tuple(range(count - 2))
    normed_refs, uppers, lowers = (normed_a, normed_b), (upper_a, upper_b), (lower_a, lower_b)

    def fetch(c):
        rows = pl.ds(c * chunk, chunk)
        return pltpu.make_async_copy(pair_hbm.at[rows], pair_scr.at[rows], sems.at[c])

    sources = (left_gate_hbm, left_proj_hbm, right_gate_hbm, right_proj_hbm)
    small = [
        pltpu.make_async_copy(source, weights_in.at[place], small_sems.at[place])
        for place, source in enumerate(sources)
    ]
    small.append(pltpu.make_async_copy(gain_hbm, gain_in, small_sems.at[4]))
    small.append(pltpu.make_async_copy(mask_hbm, mask_in, small_sems.at[5]))
    fetch(order[0]).start()
    for copy in small:
        copy.start()
    fetch(order[1]).start()
    rows = lax.broadcasted_iota(jnp.int32, (lanes, lanes), 0)
    cols = lax.broadcasted_iota(jnp.int32, (lanes, lanes), 1)
    center_scr[...] = (jnp.where(rows == cols, 1.0, 0.0) - 1.0 / lanes).astype(bf16)
    lane = lax.broadcasted_iota(jnp.int32, (1, lanes), 1)
    middle = (lane >= edge) & (lane < tile)
    spill_scr[:, 9 * 8 :, :] = jnp.zeros((part, 8, lanes), f32)
    for copy in small:
        copy.wait()
    gain = gain_in[...] * 0.5
    for place in range(4):
        scaled = weights_in[place].astype(f32) * gain
        weight_scr[place * part : (place + 1) * part, :] = scaled.astype(bf16)
    mask = mask_in[...].astype(f32)
    mask_scr[...] = jnp.concatenate([mask, mask[:, edge:]], axis=1)

    def norm(c, k, normed_ref):
        first, second = pair_scr[c * chunk + k], pair_scr[c * chunk + k + 1]
        source = jnp.concatenate([first, first[edge:], second, second[edge:]], axis=0)
        centered = lax.dot_general(center_scr[...], source, turned, preferred_element_type=f32)
        spread = jnp.sum(centered * centered, axis=0, keepdims=True) * (1.0 / lanes)
        at = c * chunk + k
        valid = jnp.concatenate([mask_scr[at : at + 1, :], mask_scr[at + 1 : at + 2, :]], axis=1)
        normed_ref[k // 2] = (centered * (lax.rsqrt(spread + epsilon) * valid)).astype(bf16)

    def values(k, normed_ref, upper, lower):
        normed = normed_ref[k // 2]
        left = jnp.dot(weight_scr[: 2 * part], normed, preferred_element_type=f32)
        right = jnp.dot(weight_scr[2 * part :], normed, preferred_element_type=f32)
        for kk in range(2):
            own = slice(kk * lanes, (kk + 1) * lanes)
            row = k + kk
            left_vals = (jnp.tanh(left[:part, own]) + 1.0) * left[part:, own]
            right_vals = (jnp.tanh(right[:part, own]) + 1.0) * right[part:, own]
            place = pl.ds(row % 8, part, stride=8)
            upper[row // 8, place, :] = jnp.where(middle, right_vals, left_vals)
            lower[row // 8, place, :] = right_vals

    def store(c, ch, upper, lower):
        def eight(ref, half):
            return ref[half, ch * 8 : (ch + 8) * 8].reshape(8, 8, lanes)

        own = slice(ch, ch + 8)
        at = c * chunk
        message_ref[own, at : at + chunk, :] = jnp.concatenate(
            [eight(upper, 0), eight(upper, 1)], axis=1
        ).astype(bf16)

        def keep(p, half):
            rows = eight(lower, half).reshape(64, lanes)
            for s in range(3):
                to = 8 * (3 * p + s)
                moved = pltpu.roll(rows, edge - 32 * s, 1)
                spill_scr[own, to : to + 8, :] = moved.reshape(8, 8, lanes)

        if c == count - 1:
            keep(1, 0)
            keep(2, 1)
        elif c == count - 2:
            keep(0, 1)
            message_ref[own, tile + at : tile + at + 8, :] = eight(lower, 0).astype(bf16)
        else:
            rows = jnp.concatenate([eight(lower, 0), eight(lower, 1)], axis=1)
            rows = jnp.where(lane[None] < edge, rows, spill_scr[own, at : at + chunk, :])
            message_ref[own, tile + at : tile + at + chunk, :] = rows.astype(bf16)

    for step in range(count + 2):
        if step == 0:
            fetch(order[0]).wait()
            for c in order[2:]:
                fetch(c).start()
        if step == 1:
            fetch(order[1]).wait()
        if step == 2:
            for c in order[2:]:
                fetch(c).wait()
        for k in range(0, chunk, 2):
            if step < count:
                norm(order[step], k, normed_refs[step % 2])
            if 1 <= step < count + 1:
                last = (step - 1) % 2
                values(k, normed_refs[last], uppers[last], lowers[last])
            if 2 <= step:
                store(order[step - 2], k * part // chunk, uppers[step % 2], lowers[step % 2])


def normalize(values, gain):
    centered = values - jnp.mean(values, axis=-1, keepdims=True)
    spread = jnp.mean(centered * centered, axis=-1, keepdims=True)
    return centered * lax.rsqrt(spread + epsilon) * gain


def sigmoid(values):
    return 0.5 * jnp.tanh(0.5 * values) + 0.5


def gate_kernel(pair_ref, gain_ref, weight_ref, gate_ref):
    half = pair_ref.shape[1] // 2
    values = pair_ref[...].astype(f32)
    own = jnp.where(lax.axis_index("ch") == 0, values[:, :half], values[:, half:])
    normed = normalize(own, gain_ref[...][None]).reshape(chunk * half, lanes).astype(bf16)
    gate = jnp.dot(normed, weight_ref[...], preferred_element_type=f32)
    gate_ref[...] = sigmoid(gate).reshape(gate_ref.shape)


def product_kernel(received_ref, out_hbm, right_a, right_b, right_c, right_d, out_scr, sems):
    rows, cols, tile = 8, 8, out_hbm.shape[1] // 8
    rights = (right_a, right_b, right_c, right_d)
    blocks_count, steps = len(rights), out_scr.shape[0]
    share, wide = cols // blocks_count, rows // steps
    lane = lax.broadcasted_iota(jnp.int32, (1, lanes), 1)

    def turn(q):
        blocks = []
        for r in range(rows):
            upper = received_ref[r * cols + q, :tile].astype(f32)
            lower = received_ref[r * cols + q, tile:].astype(f32)
            parts = [jnp.where(lane < edge, lower, upper[: tile - spill])]
            for p in range(3):
                pieces = [
                    pltpu.roll(lower[8 * (3 * p + s) : 8 * (3 * p + s) + 8], 32 * s + 32, 1)
                    for s in range(3)
                ]
                at = tile - spill + 8 * p
                eight = jnp.where(lane < edge, pieces[2], upper[at : at + 8])
                eight = jnp.where(lane < 64, pieces[1], eight)
                parts.append(jnp.where(lane < 32, pieces[0], eight))
            blocks.append(jnp.concatenate(parts, axis=0).astype(bf16))
        block = jnp.concatenate(blocks, axis=0)
        at = (q % share) * tile
        rights[q // share][at : at + tile, :] = block.T[:tile]

    def send(s, h):
        width = share * tile
        return pltpu.make_async_copy(
            out_scr.at[s, h],
            out_hbm.at[pl.ds(wide * s, wide), pl.ds(h * width, width)],
            sems.at[s, h],
        )

    def multiply(s, h):
        lefts = [
            jnp.concatenate(
                [received_ref[r * cols + wide * s + p, :tile] for r in range(rows)], axis=0
            )
            for p in range(wide)
        ]
        hidden = jnp.dot(
            rights[h][...], jnp.concatenate(lefts, axis=1), preferred_element_type=f32
        ).astype(bf16)
        for p in range(wide):
            out_scr[s, h, p] = hidden[:, p * lanes : (p + 1) * lanes]
        send(s, h).start()

    for q in range(share):
        turn(q)
    for h in range(blocks_count):
        for s in range(steps):
            if h + 1 < blocks_count:
                turn((h + 1) * share + s)
            multiply(s, h)
    for h in range(blocks_count):
        for s in range(steps):
            send(s, h).wait()


def finish_kernel(
    hidden_hbm,
    gate_ref,
    gain_ref,
    weight_ref,
    out_hbm,
    hidden_scr,
    out_scr,
    weight_scr,
    turn_a,
    turn_b,
    part_a,
    part_b,
    center_scr,
    scale_scr,
    hidden_sems,
    out_sems,
):
    groups, channels, tile = hidden_scr.shape[0], hidden_scr.shape[1], out_scr.shape[1]
    turns, outs = (turn_a, turn_b), (part_a, part_b)
    step = 16

    def fetch_hidden(g):
        return pltpu.make_async_copy(hidden_hbm.at[:, g], hidden_scr.at[g], hidden_sems.at[g])

    def send(g, n):
        own = pl.ds(n * (tile // 2), tile // 2)
        return pltpu.make_async_copy(out_scr.at[g, own], out_hbm.at[own, g], out_sems.at[g, n])

    for g in range(groups):
        fetch_hidden(g).start()
    scaled = jnp.broadcast_to(gain_ref[...], (channels, channels)).T * weight_ref[...].astype(f32)
    part = channels // 2
    for side in range(2):
        turn_a[pl.ds(side, part, stride=2), :] = scaled[side * part : (side + 1) * part]
    weight_scr[...] = turn_a[:channels, :].astype(bf16)

    def tree(terms):
        while len(terms) > 1:
            terms = [terms[n] + terms[n + 1] for n in range(0, len(terms), 2)]
        return terms[0]

    def norm(g):
        first = hidden_scr[g, 0].astype(f32)
        sums, squares = [], []
        for c in range(0, channels, step):
            moved = hidden_scr[g, c : c + step].astype(f32) - first[None]
            turns[g % 2][c * 8 : (c + step) * 8] = moved.reshape(step * 8, lanes)
            sums.append(jnp.sum(moved, axis=0))
            squares.append(jnp.sum(moved * moved, axis=0))
        center = tree(sums) * (1.0 / channels)
        spread = tree(squares) * (1.0 / channels) - center * center
        center_scr[g % 2] = center
        scale_scr[g % 2] = lax.rsqrt(jnp.maximum(spread, 0.0) + epsilon)

    def project(g, j):
        moved = turns[g % 2][pl.ds(j, channels, stride=8), :]
        center, scale = center_scr[g % 2, j : j + 1], scale_scr[g % 2, j : j + 1]
        projected = lax.dot_general(
            ((moved - center) * scale).astype(bf16),
            weight_scr[...],
            (((0,), (0,)), ((), ())),
            preferred_element_type=f32,
        )
        outs[g % 2][pl.ds(j, edge, stride=8), :] = projected[:edge]
        outs[g % 2][pl.ds(edge * 8 + j, tile - edge, stride=8), :] = projected[tile:]

    def multiply(g, n):
        count = tile // 8
        own = slice(n * count, (n + 1) * count)
        rows = outs[g % 2][n * count * 8 : (n + 1) * count * 8].reshape(count, 8, lanes)
        out_scr[g, own] = (rows * gate_ref[own, g]).astype(bf16)

    arrivals = {0: (0,), 1: (1, 2), 3: tuple(range(3, groups))}
    for s in range(groups + 2):
        for g in arrivals.get(s, ()):
            fetch_hidden(g).wait()
        if s < groups:
            norm(s)
        for j in range(8):
            if 2 <= s:
                multiply(s - 2, j)
                if j % 4 == 3:
                    send(s - 2, j // 4).start()
            if 1 <= s < groups + 1:
                project(s - 1, j)
    for g in range(groups):
        for n in range(2):
            send(g, n).wait()


def shards(
    pair,
    pair_mask,
    ln_in_gain,
    w_left_gate,
    w_left_proj,
    w_right_gate,
    w_right_proj,
    w_gate,
    ln_out_gain,
    w_out,
):
    tile, channels = pair.shape[0], pair.shape[2]
    part = w_left_gate.shape[1]
    rows, cols, ch = lax.axis_size("row"), lax.axis_size("col"), lax.axis_size("ch")
    half = tile // ch
    groups = half // 8
    limit = pltpu.CompilerParams(vmem_limit_bytes=24 * 2**20)
    vmem, anywhere = pl.BlockSpec(memory_space=pltpu.VMEM), pl.BlockSpec(memory_space=pl.ANY)
    whole = lambda shape: pl.BlockSpec(shape, lambda s: (0,) * len(shape))

    stay = lambda array: pltpu.with_memory_space_constraint(array, pltpu.HBM)
    pair = stay(pair)
    gain_row = stay(ln_in_gain.reshape(1, channels))
    weights = [stay(w.T) for w in (w_left_gate, w_left_proj, w_right_gate, w_right_proj)]
    normed_shape = pltpu.VMEM((chunk // 2, channels, 2 * lanes), bf16)
    turn_shape = pltpu.VMEM((2, part * 8, lanes), f32)
    message = pl.pallas_call(
        project_kernel,
        in_specs=[anywhere] * 7,
        out_specs=vmem,
        out_shape=jax.ShapeDtypeStruct((part, 2 * tile - spill, lanes), bf16),
        scratch_shapes=[
            pltpu.VMEM(pair_mask.shape, jnp.int32),
            pltpu.VMEM((1, channels), f32),
            pltpu.VMEM((4, part, channels), bf16),
            pltpu.VMEM(pair.shape, bf16),
            pltpu.VMEM((4 * part, channels), bf16),
            pltpu.VMEM((channels, channels), bf16),
            pltpu.VMEM((tile, lanes), f32),
            normed_shape,
            normed_shape,
            turn_shape,
            turn_shape,
            turn_shape,
            turn_shape,
            pltpu.VMEM((part, 80, lanes), f32),
            pltpu.SemaphoreType.DMA((tile // chunk,)),
            pltpu.SemaphoreType.DMA((6,)),
        ],
        compiler_params=limit,
        name="project",
    )(pair, stay(pair_mask), gain_row, *weights)

    gate = pl.pallas_call(
        gate_kernel,
        grid=(tile // chunk,),
        in_specs=[
            pl.BlockSpec((chunk, tile, channels), lambda s: (s, 0, 0)),
            whole((1, channels)),
            whole((channels, channels)),
        ],
        out_specs=pl.BlockSpec((chunk, groups, 8, lanes), lambda s: (s, 0, 0, 0)),
        out_shape=jax.ShapeDtypeStruct((tile, groups, 8, lanes), f32),
        compiler_params=limit,
        cost_estimate=pl.CostEstimate(
            flops=2 * tile * half * channels * channels,
            bytes_accessed=10 * tile * half * channels,
            transcendentals=tile * half * channels,
        ),
        name="gate",
    )(pair, gain_row, stay(w_gate))

    received = lax.all_to_all(message, ("row", "col"), 0, 0, tiled=True)

    right_shape = pltpu.VMEM((cols * tile // 4, rows * tile), bf16)
    hidden = pl.pallas_call(
        product_kernel,
        in_specs=[vmem],
        out_specs=anywhere,
        out_shape=jax.ShapeDtypeStruct((rows, cols * tile, lanes), bf16),
        scratch_shapes=[
            right_shape,
            right_shape,
            right_shape,
            right_shape,
            pltpu.VMEM((2, 4, rows // 2, cols * tile // 4, lanes), bf16),
            pltpu.SemaphoreType.DMA((2, 4)),
        ],
        compiler_params=limit,
        name="product",
    )(received)

    parts = lax.all_to_all(
        hidden.reshape(rows * cols * ch, half, lanes), ("row", "col", "ch"), 0, 0, tiled=True
    )
    parts = parts.reshape(channels, groups, 8, lanes)

    update = pl.pallas_call(
        finish_kernel,
        in_specs=[anywhere, vmem, vmem, vmem],
        out_specs=anywhere,
        out_shape=jax.ShapeDtypeStruct((tile, groups, 8, lanes), bf16),
        scratch_shapes=[
            pltpu.VMEM((groups, channels, 8, lanes), bf16),
            pltpu.VMEM((groups, tile, 8, lanes), bf16),
            pltpu.VMEM((channels, channels), bf16),
            pltpu.VMEM((channels * 8, lanes), f32),
            pltpu.VMEM((channels * 8, lanes), f32),
            pltpu.VMEM((tile * 8, lanes), f32),
            pltpu.VMEM((tile * 8, lanes), f32),
            pltpu.VMEM((2, 8, lanes), f32),
            pltpu.VMEM((2, 8, lanes), f32),
            pltpu.SemaphoreType.DMA((groups,)),
            pltpu.SemaphoreType.DMA((groups, 2)),
        ],
        compiler_params=limit,
        name="finish",
    )(parts, gate, ln_out_gain.reshape(1, channels), w_out)
    return update.reshape(tile, half, channels)


def solution(mesh):
    in_specs = (
        P("row", "col", None),
        P("row", "col"),
        P(),
        P(None, "ch"),
        P(None, "ch"),
        P(None, "ch"),
        P(None, "ch"),
        P(),
        P(),
        P(),
    )
    out_specs = P("row", ("col", "ch"), None)
    return jax.shard_map(shards, mesh=mesh, in_specs=in_specs, out_specs=out_specs, check_vma=False)
```

```python
import jax
import jax.numpy as jnp
from jax import lax
from jax.experimental import pallas as pl
from jax.experimental.pallas import tpu as pltpu
from jax.sharding import PartitionSpec as P

epsilon = 1e-05
f32 = jnp.float32
bf16 = jnp.bfloat16
lanes = 128
chunk = 16
turned = (((1,), (1,)), ((), ()))

edge = 96
spill = 24


def project_kernel(
    pair_hbm,
    mask_hbm,
    gain_hbm,
    left_gate_hbm,
    left_proj_hbm,
    right_gate_hbm,
    right_proj_hbm,
    message_ref,
    mask_in,
    gain_in,
    weights_in,
    pair_scr,
    weight_scr,
    center_scr,
    mask_scr,
    normed_a,
    normed_b,
    upper_a,
    upper_b,
    lower_a,
    lower_b,
    spill_scr,
    sems,
    small_sems,
):
    tile = pair_hbm.shape[0]
    part = left_gate_hbm.shape[0]
    count = tile // chunk
    order = (count - 1, count - 2) + tuple(range(count - 2))
    normed_refs, uppers, lowers = (normed_a, normed_b), (upper_a, upper_b), (lower_a, lower_b)

    def fetch(c):
        rows = pl.ds(c * chunk, chunk)
        return pltpu.make_async_copy(pair_hbm.at[rows], pair_scr.at[rows], sems.at[c])

    sources = (left_gate_hbm, left_proj_hbm, right_gate_hbm, right_proj_hbm)
    small = [
        pltpu.make_async_copy(source, weights_in.at[place], small_sems.at[place])
        for place, source in enumerate(sources)
    ]
    small.append(pltpu.make_async_copy(gain_hbm, gain_in, small_sems.at[4]))
    small.append(pltpu.make_async_copy(mask_hbm, mask_in, small_sems.at[5]))
    fetch(order[0]).start()
    for copy in small:
        copy.start()
    fetch(order[1]).start()
    rows = lax.broadcasted_iota(jnp.int32, (lanes, lanes), 0)
    cols = lax.broadcasted_iota(jnp.int32, (lanes, lanes), 1)
    center_scr[...] = (jnp.where(rows == cols, 1.0, 0.0) - 1.0 / lanes).astype(bf16)
    lane = lax.broadcasted_iota(jnp.int32, (1, lanes), 1)
    middle = (lane >= edge) & (lane < tile)
    spill_scr[:, 9 * 8 :, :] = jnp.zeros((part, 8, lanes), f32)
    for copy in small:
        copy.wait()
    gain = gain_in[...] * 0.5
    for place in range(4):
        scaled = weights_in[place].astype(f32) * gain
        weight_scr[place * part : (place + 1) * part, :] = scaled.astype(bf16)
    mask = mask_in[...].astype(f32)
    mask_scr[...] = jnp.concatenate([mask, mask[:, edge:]], axis=1)

    def norm(c, k, normed_ref):
        first, second = pair_scr[c * chunk + k], pair_scr[c * chunk + k + 1]
        source = jnp.concatenate([first, first[edge:], second, second[edge:]], axis=0)
        centered = lax.dot_general(center_scr[...], source, turned, preferred_element_type=f32)
        spread = jnp.sum(centered * centered, axis=0, keepdims=True) * (1.0 / lanes)
        at = c * chunk + k
        valid = jnp.concatenate([mask_scr[at : at + 1, :], mask_scr[at + 1 : at + 2, :]], axis=1)
        normed_ref[k // 2] = (centered * (lax.rsqrt(spread + epsilon) * valid)).astype(bf16)

    def values(k, normed_ref, upper, lower):
        normed = normed_ref[k // 2]
        left = jnp.dot(weight_scr[: 2 * part], normed, preferred_element_type=f32)
        right = jnp.dot(weight_scr[2 * part :], normed, preferred_element_type=f32)
        for kk in range(2):
            own = slice(kk * lanes, (kk + 1) * lanes)
            row = k + kk
            left_vals = (jnp.tanh(left[:part, own]) + 1.0) * left[part:, own]
            right_vals = (jnp.tanh(right[:part, own]) + 1.0) * right[part:, own]
            place = pl.ds(row % 8, part, stride=8)
            upper[row // 8, place, :] = jnp.where(middle, right_vals, left_vals)
            lower[row // 8, place, :] = right_vals

    def store(c, ch, upper, lower):
        def eight(ref, half):
            return ref[half, ch * 8 : (ch + 8) * 8].reshape(8, 8, lanes)

        own = slice(ch, ch + 8)
        at = c * chunk
        message_ref[own, at : at + chunk, :] = jnp.concatenate(
            [eight(upper, 0), eight(upper, 1)], axis=1
        ).astype(bf16)

        def keep(p, half):
            rows = eight(lower, half).reshape(64, lanes)
            for s in range(3):
                to = 8 * (3 * p + s)
                moved = pltpu.roll(rows, edge - 32 * s, 1)
                spill_scr[own, to : to + 8, :] = moved.reshape(8, 8, lanes)

        if c == count - 1:
            keep(1, 0)
            keep(2, 1)
        elif c == count - 2:
            keep(0, 1)
            message_ref[own, tile + at : tile + at + 8, :] = eight(lower, 0).astype(bf16)
        else:
            rows = jnp.concatenate([eight(lower, 0), eight(lower, 1)], axis=1)
            rows = jnp.where(lane[None] < edge, rows, spill_scr[own, at : at + chunk, :])
            message_ref[own, tile + at : tile + at + chunk, :] = rows.astype(bf16)

    for step in range(count + 2):
        if step == 0:
            fetch(order[0]).wait()
            for c in order[2:]:
                fetch(c).start()
        if step == 1:
            fetch(order[1]).wait()
        if step == 2:
            for c in order[2:]:
                fetch(c).wait()
        for k in range(0, chunk, 2):
            if step < count:
                norm(order[step], k, normed_refs[step % 2])
            if 1 <= step < count + 1:
                last = (step - 1) % 2
                values(k, normed_refs[last], uppers[last], lowers[last])
            if 2 <= step:
                store(order[step - 2], k * part // chunk, uppers[step % 2], lowers[step % 2])


def normalize(values, gain):
    centered = values - jnp.mean(values, axis=-1, keepdims=True)
    spread = jnp.mean(centered * centered, axis=-1, keepdims=True)
    return centered * lax.rsqrt(spread + epsilon) * gain


def sigmoid(values):
    return 0.5 * jnp.tanh(0.5 * values) + 0.5


def gate_kernel(pair_ref, gain_ref, weight_ref, gate_ref):
    half = pair_ref.shape[1] // 2
    values = pair_ref[...].astype(f32)
    own = jnp.where(lax.axis_index("ch") == 0, values[:, :half], values[:, half:])
    normed = normalize(own, gain_ref[...][None]).reshape(chunk * half, lanes).astype(bf16)
    gate = jnp.dot(normed, weight_ref[...], preferred_element_type=f32)
    gate_ref[...] = sigmoid(gate).reshape(gate_ref.shape)


def product_kernel(received_ref, out_hbm, right_a, right_b, right_c, right_d, out_scr, sems):
    ch, rows, cols, groups = out_hbm.shape[:4]
    tile = ch * groups * 8
    rights = (right_a, right_b, right_c, right_d)
    blocks_count, steps = len(rights), out_scr.shape[0]
    share, wide = cols // blocks_count, rows // steps
    lane = lax.broadcasted_iota(jnp.int32, (1, lanes), 1)

    def turn(q):
        blocks = []
        for r in range(rows):
            upper = received_ref[q * rows + r, :tile].astype(f32)
            lower = received_ref[q * rows + r, tile:].astype(f32)
            parts = [jnp.where(lane < edge, lower, upper[: tile - spill])]
            for p in range(3):
                pieces = [
                    pltpu.roll(lower[8 * (3 * p + s) : 8 * (3 * p + s) + 8], 32 * s + 32, 1)
                    for s in range(3)
                ]
                at = tile - spill + 8 * p
                eight = jnp.where(lane < edge, pieces[2], upper[at : at + 8])
                eight = jnp.where(lane < 64, pieces[1], eight)
                parts.append(jnp.where(lane < 32, pieces[0], eight))
            blocks.append(jnp.concatenate(parts, axis=0).astype(bf16))
        block = jnp.concatenate(blocks, axis=0)
        at = (q % share) * tile
        rights[q // share][at : at + tile, :] = block.T[:tile]

    def send(s, h, side):
        return pltpu.make_async_copy(
            out_scr.at[s, h, side],
            out_hbm.at[side, pl.ds(wide * s, wide), pl.ds(share * h, share)],
            sems.at[s, h, side],
        )

    def multiply(s, h):
        lefts = [
            jnp.concatenate(
                [received_ref[(wide * s + p) * rows + r, :tile] for r in range(rows)], axis=0
            )
            for p in range(wide)
        ]
        hidden = jnp.dot(
            rights[h][...], jnp.concatenate(lefts, axis=1), preferred_element_type=f32
        )
        for p in range(wide):
            own = hidden[:, p * lanes : (p + 1) * lanes].reshape(share, ch, groups, 8, lanes)
            for side in range(ch):
                out_scr[s, h, side, p] = own[:, side].astype(bf16)
        for side in range(ch):
            send(s, h, side).start()

    for q in range(share):
        turn(q)
    for h in range(blocks_count):
        for s in range(steps):
            if h + 1 < blocks_count:
                turn((h + 1) * share + s)
            multiply(s, h)
    for h in range(blocks_count):
        for s in range(steps):
            for side in range(ch):
                send(s, h, side).wait()


def finish_kernel(
    hidden_hbm,
    gate_ref,
    gain_ref,
    weight_ref,
    out_hbm,
    hidden_scr,
    out_scr,
    weight_scr,
    turn_a,
    turn_b,
    part_a,
    part_b,
    center_scr,
    scale_scr,
    hidden_sems,
    out_sems,
):
    groups, channels, tile = hidden_scr.shape[0], hidden_scr.shape[1], out_scr.shape[1]
    turns, outs = (turn_a, turn_b), (part_a, part_b)
    step = 16

    def fetch_hidden(g):
        return pltpu.make_async_copy(hidden_hbm.at[:, g], hidden_scr.at[g], hidden_sems.at[g])

    def send(g):
        return pltpu.make_async_copy(out_scr.at[g], out_hbm.at[:, g], out_sems.at[g])

    for g in range(groups):
        fetch_hidden(g).start()
    scaled = jnp.broadcast_to(gain_ref[...], (channels, channels)).T * weight_ref[...].astype(f32)
    turn_a[:channels, :] = scaled
    for at in range(0, channels, 8):
        first = at // 64 * 64 + at % 64 // 8
        turn_b[at : at + 8, :] = turn_a[pl.ds(first, 8, stride=8), :]
    weight_scr[...] = turn_b[:channels, :].astype(bf16)

    def tree(terms):
        while len(terms) > 1:
            terms = [terms[n] + terms[n + 1] for n in range(0, len(terms), 2)]
        return terms[0]

    def norm(g):
        first = hidden_scr[g, 0].astype(f32)
        sums, squares = [], []
        for c in range(0, channels, step):
            moved = hidden_scr[g, c : c + step].astype(f32) - first[None]
            turns[g % 2][c * 8 : (c + step) * 8] = moved.reshape(step * 8, lanes)
            sums.append(jnp.sum(moved, axis=0))
            squares.append(jnp.sum(moved * moved, axis=0))
        center = tree(sums) * (1.0 / channels)
        spread = tree(squares) * (1.0 / channels) - center * center
        center_scr[g % 2] = center
        scale_scr[g % 2] = lax.rsqrt(jnp.maximum(spread, 0.0) + epsilon)

    def project(g, j):
        moved = turns[g % 2][pl.ds(j, channels, stride=8), :]
        center, scale = center_scr[g % 2, j : j + 1], scale_scr[g % 2, j : j + 1]
        projected = lax.dot_general(
            ((moved - center) * scale).astype(bf16),
            weight_scr[...],
            (((0,), (0,)), ((), ())),
            preferred_element_type=f32,
        )
        outs[g % 2][pl.ds(j, edge, stride=8), :] = projected[:edge]
        outs[g % 2][pl.ds(edge * 8 + j, tile - edge, stride=8), :] = projected[tile:]

    def multiply(g, n):
        count = tile // 8
        own = slice(n * count, (n + 1) * count)
        rows = outs[g % 2][n * count * 8 : (n + 1) * count * 8].reshape(count, 8, lanes)
        out_scr[g, own] = (rows * gate_ref[own, g]).astype(bf16)

    arrivals = {0: (0,), 1: (1, 2), 3: tuple(range(3, groups))}
    for s in range(groups + 2):
        for g in arrivals.get(s, ()):
            fetch_hidden(g).wait()
        if s < groups:
            norm(s)
        for j in range(8):
            if 2 <= s:
                multiply(s - 2, j)
            if 1 <= s < groups + 1:
                project(s - 1, j)
        if 2 <= s:
            send(s - 2).start()
    for g in range(groups):
        send(g).wait()


def shards(
    pair,
    pair_mask,
    ln_in_gain,
    w_left_gate,
    w_left_proj,
    w_right_gate,
    w_right_proj,
    w_gate,
    ln_out_gain,
    w_out,
):
    tile, channels = pair.shape[0], pair.shape[2]
    part = w_left_gate.shape[1]
    rows, cols, ch = lax.axis_size("row"), lax.axis_size("col"), lax.axis_size("ch")
    half = tile // ch
    groups = half // 8
    limit = pltpu.CompilerParams(vmem_limit_bytes=24 * 2**20)
    vmem, anywhere = pl.BlockSpec(memory_space=pltpu.VMEM), pl.BlockSpec(memory_space=pl.ANY)
    whole = lambda shape: pl.BlockSpec(shape, lambda s: (0,) * len(shape))

    stay = lambda array: pltpu.with_memory_space_constraint(array, pltpu.HBM)
    pair = stay(pair)
    gain_row = stay(ln_in_gain.reshape(1, channels))
    weights = [stay(w.T) for w in (w_left_gate, w_left_proj, w_right_gate, w_right_proj)]
    normed_shape = pltpu.VMEM((chunk // 2, channels, 2 * lanes), bf16)
    turn_shape = pltpu.VMEM((2, part * 8, lanes), f32)
    message = pl.pallas_call(
        project_kernel,
        in_specs=[anywhere] * 7,
        out_specs=vmem,
        out_shape=jax.ShapeDtypeStruct((part, 2 * tile - spill, lanes), bf16),
        scratch_shapes=[
            pltpu.VMEM(pair_mask.shape, jnp.int32),
            pltpu.VMEM((1, channels), f32),
            pltpu.VMEM((4, part, channels), bf16),
            pltpu.VMEM(pair.shape, bf16),
            pltpu.VMEM((4 * part, channels), bf16),
            pltpu.VMEM((channels, channels), bf16),
            pltpu.VMEM((tile, lanes), f32),
            normed_shape,
            normed_shape,
            turn_shape,
            turn_shape,
            turn_shape,
            turn_shape,
            pltpu.VMEM((part, 80, lanes), f32),
            pltpu.SemaphoreType.DMA((tile // chunk,)),
            pltpu.SemaphoreType.DMA((6,)),
        ],
        compiler_params=limit,
        name="project",
    )(pair, stay(pair_mask), gain_row, *weights)

    gate = pl.pallas_call(
        gate_kernel,
        grid=(tile // chunk,),
        in_specs=[
            pl.BlockSpec((chunk, tile, channels), lambda s: (s, 0, 0)),
            whole((1, channels)),
            whole((channels, channels)),
        ],
        out_specs=pl.BlockSpec((chunk, groups, 8, lanes), lambda s: (s, 0, 0, 0)),
        out_shape=jax.ShapeDtypeStruct((tile, groups, 8, lanes), f32),
        compiler_params=limit,
        cost_estimate=pl.CostEstimate(
            flops=2 * tile * half * channels * channels,
            bytes_accessed=10 * tile * half * channels,
            transcendentals=tile * half * channels,
        ),
        name="gate",
    )(pair, gain_row, stay(w_gate))

    received = lax.all_to_all(message, ("col", "row"), 0, 0, tiled=True)

    right_shape = pltpu.VMEM((cols * tile // 4, rows * tile), bf16)
    hidden = pl.pallas_call(
        product_kernel,
        in_specs=[vmem],
        out_specs=anywhere,
        out_shape=jax.ShapeDtypeStruct((ch, rows, cols, groups, 8, lanes), bf16),
        scratch_shapes=[
            right_shape,
            right_shape,
            right_shape,
            right_shape,
            pltpu.VMEM((2, 4, ch, rows // 2, cols // 4, groups, 8, lanes), bf16),
            pltpu.SemaphoreType.DMA((2, 4, ch)),
        ],
        compiler_params=limit,
        name="product",
    )(received)

    parts = lax.all_to_all(
        hidden.reshape(channels, groups, 8, lanes), ("ch", "row", "col"), 0, 0, tiled=True
    )

    update = pl.pallas_call(
        finish_kernel,
        in_specs=[anywhere, vmem, vmem, vmem],
        out_specs=anywhere,
        out_shape=jax.ShapeDtypeStruct((tile, groups, 8, lanes), bf16),
        scratch_shapes=[
            pltpu.VMEM((groups, channels, 8, lanes), bf16),
            pltpu.VMEM((groups, tile, 8, lanes), bf16),
            pltpu.VMEM((channels, channels), bf16),
            pltpu.VMEM((channels * 8, lanes), f32),
            pltpu.VMEM((channels * 8, lanes), f32),
            pltpu.VMEM((tile * 8, lanes), f32),
            pltpu.VMEM((tile * 8, lanes), f32),
            pltpu.VMEM((2, 8, lanes), f32),
            pltpu.VMEM((2, 8, lanes), f32),
            pltpu.SemaphoreType.DMA((groups,)),
            pltpu.SemaphoreType.DMA((groups,)),
        ],
        compiler_params=limit,
        name="finish",
    )(parts, gate, ln_out_gain.reshape(1, channels), w_out)
    return update.reshape(tile, half, channels)


def solution(mesh):
    in_specs = (
        P("row", "col", None),
        P("row", "col"),
        P(),
        P(None, "ch"),
        P(None, "ch"),
        P(None, "ch"),
        P(None, "ch"),
        P(),
        P(),
        P(),
    )
    out_specs = P("row", ("col", "ch"), None)
    return jax.shard_map(shards, mesh=mesh, in_specs=in_specs, out_specs=out_specs, check_vma=False)
```

```python
import jax
import jax.numpy as jnp
from jax import lax
from jax.experimental import pallas as pl
from jax.experimental.pallas import tpu as pltpu
from jax.sharding import PartitionSpec as P

epsilon = 1e-05
f32 = jnp.float32
bf16 = jnp.bfloat16
lanes = 128
chunk = 16
turned = (((1,), (1,)), ((), ()))

edge = 96
spill = 24


def project_kernel(
    pair_hbm,
    mask_hbm,
    gain_hbm,
    left_gate_hbm,
    left_proj_hbm,
    right_gate_hbm,
    right_proj_hbm,
    message_ref,
    mask_in,
    gain_in,
    weights_in,
    pair_scr,
    weight_scr,
    center_scr,
    mask_scr,
    normed_a,
    normed_b,
    upper_a,
    upper_b,
    lower_a,
    lower_b,
    spill_scr,
    sems,
    small_sems,
):
    tile = pair_hbm.shape[0]
    part = left_gate_hbm.shape[0]
    count = tile // chunk
    order = (count - 1, count - 2) + tuple(range(count - 2))
    normed_refs, uppers, lowers = (normed_a, normed_b), (upper_a, upper_b), (lower_a, lower_b)

    def fetch(c):
        rows = pl.ds(c * chunk, chunk)
        return pltpu.make_async_copy(pair_hbm.at[rows], pair_scr.at[rows], sems.at[c])

    sources = (left_gate_hbm, left_proj_hbm, right_gate_hbm, right_proj_hbm)
    small = [
        pltpu.make_async_copy(source, weights_in.at[place], small_sems.at[place])
        for place, source in enumerate(sources)
    ]
    small.append(pltpu.make_async_copy(gain_hbm, gain_in, small_sems.at[4]))
    small.append(pltpu.make_async_copy(mask_hbm, mask_in, small_sems.at[5]))
    fetch(order[0]).start()
    for copy in small:
        copy.start()
    fetch(order[1]).start()
    rows = lax.broadcasted_iota(jnp.int32, (lanes, lanes), 0)
    cols = lax.broadcasted_iota(jnp.int32, (lanes, lanes), 1)
    center_scr[...] = (jnp.where(rows == cols, 1.0, 0.0) - 1.0 / lanes).astype(bf16)
    lane = lax.broadcasted_iota(jnp.int32, (1, lanes), 1)
    middle = (lane >= edge) & (lane < tile)
    spill_scr[:, 9 * 8 :, :] = jnp.zeros((part, 8, lanes), f32)
    for copy in small:
        copy.wait()
    gain = gain_in[...] * 0.5
    for place in range(4):
        scaled = weights_in[place].astype(f32) * gain
        weight_scr[place * part : (place + 1) * part, :] = scaled.astype(bf16)
    mask = mask_in[...].astype(f32)
    mask_scr[...] = jnp.concatenate([mask, mask[:, edge:]], axis=1)

    def norm(c, k, normed_ref):
        first, second = pair_scr[c * chunk + k], pair_scr[c * chunk + k + 1]
        source = jnp.concatenate([first, first[edge:], second, second[edge:]], axis=0)
        centered = lax.dot_general(center_scr[...], source, turned, preferred_element_type=f32)
        spread = jnp.sum(centered * centered, axis=0, keepdims=True) * (1.0 / lanes)
        at = c * chunk + k
        valid = jnp.concatenate([mask_scr[at : at + 1, :], mask_scr[at + 1 : at + 2, :]], axis=1)
        normed_ref[k // 2] = (centered * (lax.rsqrt(spread + epsilon) * valid)).astype(bf16)

    def values(k, normed_ref, upper, lower):
        normed = normed_ref[k // 2]
        left = jnp.dot(weight_scr[: 2 * part], normed, preferred_element_type=f32)
        right = jnp.dot(weight_scr[2 * part :], normed, preferred_element_type=f32)
        for kk in range(2):
            own = slice(kk * lanes, (kk + 1) * lanes)
            row = k + kk
            left_vals = (jnp.tanh(left[:part, own]) + 1.0) * left[part:, own]
            right_vals = (jnp.tanh(right[:part, own]) + 1.0) * right[part:, own]
            place = pl.ds(row % 8, part, stride=8)
            upper[row // 8, place, :] = jnp.where(middle, right_vals, left_vals)
            lower[row // 8, place, :] = right_vals

    def store(c, ch, upper, lower):
        def eight(ref, half):
            return ref[half, ch * 8 : (ch + 8) * 8].reshape(8, 8, lanes)

        own = slice(ch, ch + 8)
        at = c * chunk
        message_ref[own, at : at + chunk, :] = jnp.concatenate(
            [eight(upper, 0), eight(upper, 1)], axis=1
        ).astype(bf16)

        def keep(p, half):
            rows = eight(lower, half).reshape(64, lanes)
            for s in range(3):
                to = 8 * (3 * p + s)
                moved = pltpu.roll(rows, edge - 32 * s, 1)
                spill_scr[own, to : to + 8, :] = moved.reshape(8, 8, lanes)

        if c == count - 1:
            keep(1, 0)
            keep(2, 1)
        elif c == count - 2:
            keep(0, 1)
            message_ref[own, tile + at : tile + at + 8, :] = eight(lower, 0).astype(bf16)
        else:
            rows = jnp.concatenate([eight(lower, 0), eight(lower, 1)], axis=1)
            rows = jnp.where(lane[None] < edge, rows, spill_scr[own, at : at + chunk, :])
            message_ref[own, tile + at : tile + at + chunk, :] = rows.astype(bf16)

    for step in range(count + 2):
        if step == 0:
            fetch(order[0]).wait()
            for c in order[2:]:
                fetch(c).start()
        if step == 1:
            fetch(order[1]).wait()
        if step == 2:
            for c in order[2:]:
                fetch(c).wait()
        for k in range(0, chunk, 2):
            if step < count:
                norm(order[step], k, normed_refs[step % 2])
            if 1 <= step < count + 1:
                last = (step - 1) % 2
                values(k, normed_refs[last], uppers[last], lowers[last])
            if 2 <= step:
                store(order[step - 2], k * part // chunk, uppers[step % 2], lowers[step % 2])


def normalize(values, gain):
    centered = values - jnp.mean(values, axis=-1, keepdims=True)
    spread = jnp.mean(centered * centered, axis=-1, keepdims=True)
    return centered * lax.rsqrt(spread + epsilon) * gain


def sigmoid(values):
    return 0.5 * jnp.tanh(0.5 * values) + 0.5


def gate_kernel(pair_ref, gain_ref, weight_ref, gate_ref):
    half = pair_ref.shape[1] // 2
    values = pair_ref[...].astype(f32)
    own = jnp.where(lax.axis_index("ch") == 0, values[:, :half], values[:, half:])
    normed = normalize(own, gain_ref[...][None]).reshape(chunk * half, lanes).astype(bf16)
    gate = jnp.dot(normed, weight_ref[...], preferred_element_type=f32)
    gate_ref[...] = sigmoid(gate).reshape(gate_ref.shape)


def product_kernel(received_ref, out_hbm, right_a, right_b, right_c, right_d, out_scr, sems):
    ch, rows, cols, groups = out_hbm.shape[:4]
    tile = ch * groups * 8
    rights = (right_a, right_b, right_c, right_d)
    blocks_count, steps = len(rights), out_scr.shape[0]
    share, wide = cols // blocks_count, rows // steps
    lane = lax.broadcasted_iota(jnp.int32, (1, lanes), 1)

    def turn(q):
        blocks = []
        for r in range(rows):
            upper = received_ref[r * cols + q, :tile].astype(f32)
            lower = received_ref[r * cols + q, tile:].astype(f32)
            parts = [jnp.where(lane < edge, lower, upper[: tile - spill])]
            for p in range(3):
                pieces = [
                    pltpu.roll(lower[8 * (3 * p + s) : 8 * (3 * p + s) + 8], 32 * s + 32, 1)
                    for s in range(3)
                ]
                at = tile - spill + 8 * p
                eight = jnp.where(lane < edge, pieces[2], upper[at : at + 8])
                eight = jnp.where(lane < 64, pieces[1], eight)
                parts.append(jnp.where(lane < 32, pieces[0], eight))
            blocks.append(jnp.concatenate(parts, axis=0).astype(bf16))
        block = jnp.concatenate(blocks, axis=0)
        at = (q % share) * tile
        rights[q // share][at : at + tile, :] = block.T[:tile]

    def send(s, h, side):
        return pltpu.make_async_copy(
            out_scr.at[s, h, side],
            out_hbm.at[side, pl.ds(wide * s, wide), pl.ds(share * h, share)],
            sems.at[s, h, side],
        )

    def multiply(s, h):
        lefts = [
            jnp.concatenate(
                [received_ref[r * cols + wide * s + p, :tile] for r in range(rows)], axis=0
            )
            for p in range(wide)
        ]
        hidden = jnp.dot(
            rights[h][...], jnp.concatenate(lefts, axis=1), preferred_element_type=f32
        )
        for p in range(wide):
            own = hidden[:, p * lanes : (p + 1) * lanes].reshape(share, ch, groups, 8, lanes)
            for side in range(ch):
                out_scr[s, h, side, p] = own[:, side].astype(bf16)
        for side in range(ch):
            send(s, h, side).start()

    for q in range(share):
        turn(q)
    for h in range(blocks_count):
        for s in range(steps):
            if h + 1 < blocks_count:
                turn((h + 1) * share + s)
            multiply(s, h)
    for h in range(blocks_count):
        for s in range(steps):
            for side in range(ch):
                send(s, h, side).wait()


def finish_kernel(
    hidden_hbm,
    gate_ref,
    gain_ref,
    weight_ref,
    out_hbm,
    hidden_scr,
    out_scr,
    weight_scr,
    turn_a,
    turn_b,
    part_a,
    part_b,
    center_scr,
    scale_scr,
    hidden_sems,
    out_sems,
):
    groups, channels, tile = hidden_scr.shape[0], hidden_scr.shape[1], out_scr.shape[1]
    turns, outs = (turn_a, turn_b), (part_a, part_b)
    step = 16

    def fetch_hidden(g):
        return pltpu.make_async_copy(hidden_hbm.at[:, g], hidden_scr.at[g], hidden_sems.at[g])

    def send(g, n):
        own = pl.ds(n * (tile // 2), tile // 2)
        return pltpu.make_async_copy(out_scr.at[g, own], out_hbm.at[own, g], out_sems.at[g, n])

    for g in range(groups):
        fetch_hidden(g).start()
    scaled = jnp.broadcast_to(gain_ref[...], (channels, channels)).T * weight_ref[...].astype(f32)
    weight_scr[...] = scaled.astype(bf16)

    def tree(terms):
        while len(terms) > 1:
            terms = [terms[n] + terms[n + 1] for n in range(0, len(terms), 2)]
        return terms[0]

    def norm(g):
        first = hidden_scr[g, 0].astype(f32)
        sums, squares = [], []
        for c in range(0, channels, step):
            moved = hidden_scr[g, c : c + step].astype(f32) - first[None]
            turns[g % 2][c * 8 : (c + step) * 8] = moved.reshape(step * 8, lanes)
            sums.append(jnp.sum(moved, axis=0))
            squares.append(jnp.sum(moved * moved, axis=0))
        center = tree(sums) * (1.0 / channels)
        spread = tree(squares) * (1.0 / channels) - center * center
        center_scr[g % 2] = center
        scale_scr[g % 2] = lax.rsqrt(jnp.maximum(spread, 0.0) + epsilon)

    def project(g, j):
        moved = turns[g % 2][pl.ds(j, channels, stride=8), :]
        center, scale = center_scr[g % 2, j : j + 1], scale_scr[g % 2, j : j + 1]
        projected = lax.dot_general(
            ((moved - center) * scale).astype(bf16),
            weight_scr[...],
            (((0,), (0,)), ((), ())),
            preferred_element_type=f32,
        )
        outs[g % 2][pl.ds(j, edge, stride=8), :] = projected[:edge]
        outs[g % 2][pl.ds(edge * 8 + j, tile - edge, stride=8), :] = projected[tile:]

    def multiply(g, n):
        count = tile // 8
        own = slice(n * count, (n + 1) * count)
        rows = outs[g % 2][n * count * 8 : (n + 1) * count * 8].reshape(count, 8, lanes)
        out_scr[g, own] = (rows * gate_ref[own, g]).astype(bf16)

    arrivals = {0: (0,), 1: (1, 2), 3: tuple(range(3, groups))}
    for s in range(groups + 2):
        for g in arrivals.get(s, ()):
            fetch_hidden(g).wait()
        if s < groups:
            norm(s)
        for j in range(8):
            if 2 <= s:
                multiply(s - 2, j)
                if j % 4 == 3:
                    send(s - 2, j // 4).start()
            if 1 <= s < groups + 1:
                project(s - 1, j)
    for g in range(groups):
        for n in range(2):
            send(g, n).wait()


def shards(
    pair,
    pair_mask,
    ln_in_gain,
    w_left_gate,
    w_left_proj,
    w_right_gate,
    w_right_proj,
    w_gate,
    ln_out_gain,
    w_out,
):
    tile, channels = pair.shape[0], pair.shape[2]
    part = w_left_gate.shape[1]
    rows, cols, ch = lax.axis_size("row"), lax.axis_size("col"), lax.axis_size("ch")
    half = tile // ch
    groups = half // 8
    limit = pltpu.CompilerParams(vmem_limit_bytes=24 * 2**20)
    vmem, anywhere = pl.BlockSpec(memory_space=pltpu.VMEM), pl.BlockSpec(memory_space=pl.ANY)
    whole = lambda shape: pl.BlockSpec(shape, lambda s: (0,) * len(shape))

    stay = lambda array: pltpu.with_memory_space_constraint(array, pltpu.HBM)
    pair = stay(pair)
    gain_row = stay(ln_in_gain.reshape(1, channels))
    weights = [stay(w.T) for w in (w_left_gate, w_left_proj, w_right_gate, w_right_proj)]
    normed_shape = pltpu.VMEM((chunk // 2, channels, 2 * lanes), bf16)
    turn_shape = pltpu.VMEM((2, part * 8, lanes), f32)
    message = pl.pallas_call(
        project_kernel,
        in_specs=[anywhere] * 7,
        out_specs=vmem,
        out_shape=jax.ShapeDtypeStruct((part, 2 * tile - spill, lanes), bf16),
        scratch_shapes=[
            pltpu.VMEM(pair_mask.shape, jnp.int32),
            pltpu.VMEM((1, channels), f32),
            pltpu.VMEM((4, part, channels), bf16),
            pltpu.VMEM(pair.shape, bf16),
            pltpu.VMEM((4 * part, channels), bf16),
            pltpu.VMEM((channels, channels), bf16),
            pltpu.VMEM((tile, lanes), f32),
            normed_shape,
            normed_shape,
            turn_shape,
            turn_shape,
            turn_shape,
            turn_shape,
            pltpu.VMEM((part, 80, lanes), f32),
            pltpu.SemaphoreType.DMA((tile // chunk,)),
            pltpu.SemaphoreType.DMA((6,)),
        ],
        compiler_params=limit,
        name="project",
    )(pair, stay(pair_mask), gain_row, *weights)

    gate = pl.pallas_call(
        gate_kernel,
        grid=(tile // chunk,),
        in_specs=[
            pl.BlockSpec((chunk, tile, channels), lambda s: (s, 0, 0)),
            whole((1, channels)),
            whole((channels, channels)),
        ],
        out_specs=pl.BlockSpec((chunk, groups, 8, lanes), lambda s: (s, 0, 0, 0)),
        out_shape=jax.ShapeDtypeStruct((tile, groups, 8, lanes), f32),
        compiler_params=limit,
        cost_estimate=pl.CostEstimate(
            flops=2 * tile * half * channels * channels,
            bytes_accessed=10 * tile * half * channels,
            transcendentals=tile * half * channels,
        ),
        name="gate",
    )(pair, gain_row, stay(w_gate))

    received = lax.all_to_all(message, ("row", "col"), 0, 0, tiled=True)

    right_shape = pltpu.VMEM((cols * tile // 4, rows * tile), bf16)
    hidden = pl.pallas_call(
        product_kernel,
        in_specs=[vmem],
        out_specs=anywhere,
        out_shape=jax.ShapeDtypeStruct((ch, rows, cols, groups, 8, lanes), bf16),
        scratch_shapes=[
            right_shape,
            right_shape,
            right_shape,
            right_shape,
            pltpu.VMEM((2, 4, ch, rows // 2, cols // 4, groups, 8, lanes), bf16),
            pltpu.SemaphoreType.DMA((2, 4, ch)),
        ],
        compiler_params=limit,
        name="product",
    )(received)

    parts = lax.all_to_all(
        hidden.reshape(channels, groups, 8, lanes), ("ch", "row", "col"), 0, 0, tiled=True
    )

    update = pl.pallas_call(
        finish_kernel,
        in_specs=[anywhere, vmem, vmem, vmem],
        out_specs=anywhere,
        out_shape=jax.ShapeDtypeStruct((tile, groups, 8, lanes), bf16),
        scratch_shapes=[
            pltpu.VMEM((groups, channels, 8, lanes), bf16),
            pltpu.VMEM((groups, tile, 8, lanes), bf16),
            pltpu.VMEM((channels, channels), bf16),
            pltpu.VMEM((channels * 8, lanes), f32),
            pltpu.VMEM((channels * 8, lanes), f32),
            pltpu.VMEM((tile * 8, lanes), f32),
            pltpu.VMEM((tile * 8, lanes), f32),
            pltpu.VMEM((2, 8, lanes), f32),
            pltpu.VMEM((2, 8, lanes), f32),
            pltpu.SemaphoreType.DMA((groups,)),
            pltpu.SemaphoreType.DMA((groups, 2)),
        ],
        compiler_params=limit,
        name="finish",
    )(parts, gate, ln_out_gain.reshape(1, channels), w_out)
    return update.reshape(tile, half, channels)


def solution(mesh):
    in_specs = (
        P("row", "col", None),
        P("row", "col"),
        P(),
        P(None, "ch"),
        P(None, "ch"),
        P(None, "ch"),
        P(None, "ch"),
        P(),
        P(),
        P(),
    )
    out_specs = P("row", ("col", "ch"), None)
    return jax.shard_map(shards, mesh=mesh, in_specs=in_specs, out_specs=out_specs, check_vma=False)
```
